128 devices in a mesh: rows: 16 (over x, z), grp: 8 (over y, core).
Axes of the slice: x: 4, y: 4, z: 4, core: 2. Of those that a mesh axis runs over, the one named last changes fastest.
Arguments:
- bin_codes: int32 [524288, 512], P(('rows', 'grp')), may hold values from 0 to 31
- leaf_index: int32 [524288, 1], P(('rows', 'grp')), may hold values from 0 to 7; in each aligned block of 4096 rows (0 to 4095, 4096 to 8191, ...) at most 1024 rows name the same one
- gradients: bfloat16 [524288, 16], P(('rows', 'grp')), may hold values from -6 to 6
- row_weights: bfloat16 [524288], P(('rows', 'grp')), may hold values from 0.5 to 2
- split_feature: int32 [1], replicated, may hold values from 0 to 511
- split_bin: int32 [1], replicated, may hold values from 0 to 30
Outputs:
- gain_table: float32 [16384], P('rows')
- best_gain: float32 [1], replicated
- moved_gradients: bfloat16 [128, 131072], P(('rows', 'grp'))
- moved_weights: bfloat16 [128, 8192], P(('rows', 'grp'))
The draws below stay inside these ranges and needn't reach their ends.
Inputs may be any that keep to these rules, and one draw needn't show every extreme that they name: `leaf_index`: among the rows of one device, each leaf holds at most 1024 rows, and some leaf holds exactly 1024 on some devices.
All inputs are finite; a program needn't handle non-finite values.
Results may differ from the reference program's by a relative error of at most 0.0004.
Values may be sent and summed in bfloat16 or wider, within the bound.
No kernel may reach another device: no remote copies, remote signals or barrier semaphores. Data moves between devices by JAX's collectives and lax.ppermute only.
A program may use at most 128 MiB of HBM per device.

```python
import math
import jax
import jax.numpy as jnp
import numpy as np
from jax import lax

FEATURES = 512
BINS = 32
TARGETS = 16
LEAVES = 8
ROW_DEV = 4096
CAP = 1024
TOTAL_ROWS = 524288
N_ROWS = 16
N_GRP = 8


def touch_ends(array, own_key, smallest, top_value):
    longest = array.shape.index(max(array.shape))
    spots = []
    for shift in (0, 1):
        where = [jax.random.randint(jax.random.fold_in(own_key, axis), (), 0, length) for axis, length in enumerate(array.shape)]
        where[longest] = (where[longest] + shift) % array.shape[longest]
        spots.append(tuple(where))
    return array.at[spots[0]].set(smallest).at[spots[1]].set(top_value)


def levels(stream_key, extent, pieces, low, high):
    gain, own = 1.0, jax.random.fold_in(stream_key, 6)
    for axis_at, shards_of in pieces:
        steps = jnp.exp(jax.random.uniform(jax.random.fold_in(own, axis_at), (shards_of,), jnp.float32, low / len(pieces), high / len(pieces)))
        gain = gain * jnp.repeat(steps, extent[axis_at] // shards_of).reshape([-1 if axis == axis_at else 1 for axis in range(len(extent))])
    return gain


def assign_block(stream_key, own, number, rows, amount, top, limit, slope):
    ranking = jax.random.permutation(stream_key, amount)
    crowded, usual = load_shares(amount, rows * top, limit, slope, True), load_shares(amount, rows * top, limit, slope, False)
    places = jnp.arange(amount)

    def named(sizes, turn):
        used = int((sizes > 0).sum())
        fixed = max(1, used // 4)
        passed = fixed + (places - fixed + turn * (used - fixed)) % max(1, amount - fixed)
        return jnp.zeros((amount,), jnp.int32).at[ranking[jnp.where(places < fixed, places, passed)]].set(jnp.asarray(sizes, jnp.int32))

    sizes = jnp.where(number % 4 == 0, named(crowded, number // 4), named(usual, number - number // 4 - 1))
    mixed = jax.random.permutation(jax.random.fold_in(own, 3), amount)
    donor, receiver = mixed[0:amount // 2 * 2:2], mixed[1:amount // 2 * 2:2]
    slack = jnp.minimum(sizes[donor] - 1, limit - sizes[receiver]) // 2
    slack = jnp.where((donor == ranking[0]) | (receiver == ranking[0]) | (sizes[receiver] == 0), 0, jnp.maximum(slack, 0))
    passed = jax.random.randint(jax.random.fold_in(own, 4), (amount // 2,), 0, 1 << 20) % (slack + 1)
    sizes = sizes.at[donor].add(-passed).at[receiver].add(passed)
    members = jnp.searchsorted(jnp.cumsum(sizes), jnp.arange(rows * top), side="right").astype(jnp.int32)
    listing = members.reshape(top, rows).T
    listing = listing[jax.random.permutation(jax.random.fold_in(own, 1), rows)]
    turn = jax.random.randint(jax.random.fold_in(own, 2), (rows, 1), 0, top)
    return jnp.take_along_axis(listing, (jnp.arange(top)[None, :] + turn) % top, axis=1)


def load_shares(amount, total, most, lean, full):
    weights = [(1 << 20) // math.isqrt(rank ** lean) + 1 for rank in range(1, amount + 1)]
    largest = most if full else min(most, max(-(-total // amount), total * weights[0] // sum(weights)))
    least = 1 if total - largest >= amount - 1 else 0
    given, rest = [largest] + [least] * (amount - 1), total - largest - least * (amount - 1)
    while rest > 0:
        candidates = [i for i in range(1, amount) if given[i] < largest] or [i for i in range(1, amount) if given[i] < most]
        whole, budget = sum([weights[i] for i in candidates]), rest
        for i in candidates:
            addition = min(most - given[i], max(1, budget * weights[i] // whole), rest)
            given[i] = given[i] + addition
            rest = rest - addition
    return np.array(given)


def bell_draw(stream_key, shape, scale, most, split=(), kind=jnp.bfloat16):
    array = jax.random.normal(stream_key, shape, jnp.float32) * scale
    if len(split) > 0:
        array = levels(stream_key, shape, split, -0.22, 0.18) * array
    return jnp.clip(array, min=-most, max=most).astype(kind)


def setup_inputs(seed: int = 0) -> dict:
    arg_keys = jax.random.split(jax.random.key(seed), 7)
    bin_codes = touch_ends(jax.random.randint(arg_keys[0], (TOTAL_ROWS, FEATURES), 0, BINS), jax.random.fold_in(arg_keys[0], 1), 0, BINS - 1).astype(jnp.int32)
    leaf_index_keys = jax.random.split(jax.random.fold_in(arg_keys[1], 1), TOTAL_ROWS // ROW_DEV)
    leaf_index_turns = jax.random.permutation(jax.random.fold_in(arg_keys[1], 3), TOTAL_ROWS // ROW_DEV)
    leaf_index = jax.vmap(lambda own, number: assign_block(jax.random.fold_in(arg_keys[1], 2), own, number, ROW_DEV, LEAVES, 1, CAP, 2))(leaf_index_keys, leaf_index_turns).reshape((TOTAL_ROWS, 1))
    gradients = bell_draw(arg_keys[2], (TOTAL_ROWS, TARGETS), 1.0, 6.0, ((0, 128),))
    row_weights = jnp.clip(jnp.exp(math.log(2.0) - 1.3862944 * jax.random.uniform(arg_keys[3], (TOTAL_ROWS,), jnp.float32) ** levels(arg_keys[3], (TOTAL_ROWS,), ((0, 128),), -0.2, 0.2)), 0.5, 2.0).astype(jnp.bfloat16)
    split_feature = jax.random.randint(arg_keys[4], (1,), 0, FEATURES).astype(jnp.int32)
    split_bin = jax.random.randint(arg_keys[5], (1,), 0, BINS - 1).astype(jnp.int32)
    return {"bin_codes": bin_codes, "leaf_index": leaf_index, "gradients": gradients, "row_weights": row_weights, "split_feature": split_feature, "split_bin": split_bin}


ridge = 1.0


def split_scores(grad_hist, weight_hist):
    left_g = jnp.cumsum(grad_hist, axis=1)
    left_w = jnp.cumsum(weight_hist, axis=1)
    upper_g = jnp.flip(jnp.cumsum(jnp.flip(grad_hist, axis=1), axis=1), axis=1)
    upper_w = jnp.flip(jnp.cumsum(jnp.flip(weight_hist, axis=1), axis=1), axis=1)
    right_g = jnp.concatenate([upper_g[:, 1:], jnp.zeros_like(upper_g[:, :1])], axis=1)
    right_w = jnp.concatenate([upper_w[:, 1:], jnp.zeros_like(upper_w[:, :1])], axis=1)
    left_x = left_w + ridge
    right_y = right_w + ridge
    diff = left_g * right_y[..., None] - right_g * left_x[..., None]
    terms = diff * diff / (left_x * right_y * (left_x + right_y))[..., None]
    return jnp.sum(terms, axis=(2, 3)) / (LEAVES * TARGETS)


def place_rows(leaf, child, grads, weights):
    key_ids = leaf * 2 + child
    key_hot = (key_ids[:, None] == jnp.arange(2 * LEAVES, dtype=jnp.int32)[None, :]).astype(jnp.int32)
    before = jnp.cumsum(key_hot, axis=0) - key_hot
    rank = jnp.sum(before * key_hot, axis=1)
    counts = jnp.sum(key_hot, axis=0)
    leaf_hot = (leaf[:, None] == jnp.arange(LEAVES, dtype=jnp.int32)[None, :]).astype(jnp.int32)
    first = jnp.sum(leaf_hot * counts[0::2][None, :], axis=1)
    slot = (leaf * CAP + rank + child * first).astype(jnp.int32)
    buf_g = jnp.zeros((LEAVES * CAP, grads.shape[1]), grads.dtype).at[slot].set(grads)
    buf_w = jnp.zeros((LEAVES * CAP,), weights.dtype).at[slot].set(weights)
    return buf_g.reshape(LEAVES, CAP * grads.shape[1]), buf_w.reshape(LEAVES, CAP)


def reference(bin_codes, leaf_index, gradients, row_weights, split_feature, split_bin):
    leaf = leaf_index[:, 0]
    data = jnp.concatenate([gradients.astype(jnp.float32), row_weights.astype(jnp.float32)[:, None]], axis=1)

    def one_feature(index):
        column = lax.dynamic_slice_in_dim(bin_codes, index, 1, 1)[:, 0]
        return jax.ops.segment_sum(data, column * LEAVES + leaf, num_segments=BINS * LEAVES)

    hist = lax.map(one_feature, jnp.arange(FEATURES, dtype=jnp.int32))
    hist = hist.reshape(FEATURES, BINS, LEAVES, TARGETS + 1)
    gain_table = split_scores(hist[..., :TARGETS], hist[..., TARGETS]).reshape(FEATURES * BINS)
    best_gain = jnp.max(gain_table).reshape(1)
    column = lax.dynamic_slice_in_dim(bin_codes, split_feature[0].astype(jnp.int32), 1, 1)[:, 0]
    child = (column > split_bin[0]).astype(jnp.int32)
    blocks = N_ROWS * N_GRP
    buf_g, buf_w = jax.vmap(place_rows)(leaf.reshape(blocks, ROW_DEV), child.reshape(blocks, ROW_DEV),
                                        gradients.reshape(blocks, ROW_DEV, TARGETS), row_weights.reshape(blocks, ROW_DEV))
    moved_gradients = buf_g.reshape(N_ROWS, N_GRP, LEAVES, CAP * TARGETS).transpose(0, 2, 1, 3).reshape(N_ROWS * LEAVES, N_GRP * CAP * TARGETS)
    moved_weights = buf_w.reshape(N_ROWS, N_GRP, LEAVES, CAP).transpose(0, 2, 1, 3).reshape(N_ROWS * LEAVES, N_GRP * CAP)
    return gain_table, best_gain, moved_gradients, moved_weights
```

```python
import functools

import jax
import jax.numpy as jnp
from jax import lax
from jax.experimental import pallas as pl
from jax.experimental.pallas import tpu as pltpu
from jax.sharding import Mesh
from jax.sharding import PartitionSpec as P

BINS = 32
TARGETS = 16
LEAVES = 8
CAP = 1024
COLS = LEAVES * TARGETS
FEATURES = 512
HALF = FEATURES // 2
ROW_DEV = 4096
ROW_BLOCK = 512
PEERS = 64
OWNED = 4
PAIRS = BINS // 2
AUX = 32
AUX_CHUNK = HALF
AUX_ROWS = ROW_DEV // AUX_CHUNK * AUX
LANES = 2 * HALF
SENT = COLS + LEAVES
GRP = ("grp_0", "grp_1")
ROWS_GRP = ("rows_0", "rows_1", "grp_0", "grp_1")
ROWS = ("rows_0", "rows_1")
CHIPS = ("rows_0", "rows_1", "grp_0")
VMEM = 56 << 20
F32 = jnp.float32
BF16 = jnp.bfloat16
I32 = jnp.int32


def iota(shape, dim):
    return lax.broadcasted_iota(I32, shape, dim)


def params(**more):
    return pltpu.CompilerParams(vmem_limit_bytes=VMEM, **more)


def prep_kernel(core_ref, feature_ref, codes_ref, aux_ref, own_ref, send_ref, column_ref, select_ref):
    step = pl.program_id(0)
    blocks = ROW_DEV // ROW_BLOCK

    @pl.when(step == 0)
    def _():
        core = core_ref[0]
        lane = iota((FEATURES, FEATURES), 1)
        side = jnp.where(lane < HALF, core, 1 - core)
        place = lax.rem(lane, HALF)
        wanted = (place // OWNED) * (2 * OWNED) + side * OWNED + lax.rem(place, OWNED)
        select_ref[...] = jnp.where(iota((FEATURES, FEATURES), 0) == wanted, 1.0, 0.0).astype(BF16)

    @pl.when(step < blocks)
    def _():
        codes = codes_ref[...].astype(F32).astype(BF16)
        both = jnp.dot(codes, select_ref[...], preferred_element_type=F32).astype(BF16)
        own_ref[...] = both[:, :HALF]
        send_ref[...] = both[:, HALF:]
        hot = jnp.where(iota((8, FEATURES), 1) == feature_ref[0], 1.0, 0.0).astype(BF16)
        column_ref[...] = lax.dot_general(
            hot, codes, (((1,), (1,)), ((), ())), preferred_element_type=F32
        )

    @pl.when(step == blocks)
    def _():
        for i in range(ROW_DEV // AUX_CHUNK):
            part = aux_ref[:, i * AUX_CHUNK : (i + 1) * AUX_CHUNK]
            own_ref[i * AUX : (i + 1) * AUX, :] = part
            send_ref[i * AUX : (i + 1) * AUX, :] = part


def prep(core, split_feature, codes, aux):
    blocks = ROW_DEV // ROW_BLOCK
    smem = pl.BlockSpec(memory_space=pltpu.SMEM)
    buffer = jax.ShapeDtypeStruct((ROW_DEV + AUX_ROWS, HALF), BF16)
    return pl.pallas_call(
        prep_kernel,
        grid=(blocks + 1,),
        in_specs=[
            smem,
            smem,
            pl.BlockSpec((ROW_BLOCK, FEATURES), lambda i: (jnp.minimum(i, blocks - 1), 0)),
            pl.BlockSpec((AUX, ROW_DEV), lambda i: (0, 0)),
        ],
        out_specs=[
            pl.BlockSpec((ROW_BLOCK, HALF), lambda i: (i, 0)),
            pl.BlockSpec((ROW_BLOCK, HALF), lambda i: (i, 0)),
            pl.BlockSpec((8, ROW_BLOCK), lambda i: (0, jnp.minimum(i, blocks - 1))),
        ],
        out_shape=[buffer, buffer, jax.ShapeDtypeStruct((8, ROW_DEV), F32)],
        scratch_shapes=[pltpu.VMEM((FEATURES, FEATURES), BF16)],
        compiler_params=params(),
        cost_estimate=pl.CostEstimate(
            flops=2 * ROW_DEV * FEATURES * FEATURES,
            bytes_accessed=ROW_DEV * FEATURES * 6,
            transcendentals=0,
        ),
    )(core, split_feature, codes, aux)


def unpack_aux(rows_ref):
    parts = [
        rows_ref[ROW_DEV + i * AUX : ROW_DEV + (i + 1) * AUX, :]
        for i in range(ROW_DEV // AUX_CHUNK)
    ]
    return jnp.concatenate(parts, axis=1).astype(F32)


def spread(rows_ref, dup_ref, data_ref):
    lane = iota((HALF, LANES), 1)
    source = (lane // (2 * OWNED)) * OWNED + lax.rem(lane, OWNED)
    twice = jnp.where(iota((HALF, LANES), 0) == source, 1.0, 0.0).astype(BF16)
    for i in range(ROW_DEV // ROW_BLOCK):
        rows = slice(i * ROW_BLOCK, (i + 1) * ROW_BLOCK)
        dup_ref[rows, :] = jnp.dot(
            rows_ref[rows, :], twice, preferred_element_type=F32
        ).astype(BF16)
    aux = unpack_aux(rows_ref)
    grads, weights, leaf = (aux[:TARGETS], aux[TARGETS : TARGETS + 1], aux[TARGETS + 1 : TARGETS + 2])
    for l in range(LEAVES):
        data_ref[l * TARGETS : (l + 1) * TARGETS, :] = jnp.where(leaf == l, grads, 0.0).astype(BF16)
    ids = iota((TARGETS, ROW_DEV), 0).astype(F32)
    data_ref[COLS : COLS + TARGETS, :] = jnp.where(leaf == ids, weights, 0.0).astype(BF16)


def pair_sums(pair, dup_ref, data_ref):
    lane = iota((1, LANES), 1)
    wanted = (2 * pair + lax.rem(lane // OWNED, 2)).astype(F32).astype(BF16)
    hot = jnp.where(dup_ref[...] == wanted, jnp.ones((), BF16), jnp.zeros((), BF16))
    return jnp.dot(data_ref[...], hot, preferred_element_type=F32)[:SENT]


UNROLL = 2


def own_kernel(rows_ref, sums_ref, dup_ref, data_ref):
    step = pl.program_id(0)

    @pl.when(step == 0)
    def _():
        spread(rows_ref, dup_ref, data_ref)

    for i in range(UNROLL):
        sums_ref[i] = pair_sums(step * UNROLL + i, dup_ref, data_ref)


def both_kernel(rows_ref, sums_ref, out_ref, dup_ref, data_ref, weights_ref):
    step = pl.program_id(0)

    @pl.when(step == 0)
    def _():
        spread(rows_ref, dup_ref, data_ref)

    for i in range(UNROLL):
        pair = step * UNROLL + i
        sums = pair_sums(pair, dup_ref, data_ref) + sums_ref[i]
        at = pl.multiple_of(pair * 8, 8)
        out_ref[:, pl.ds(at, 8), :] = sums[:COLS].T.reshape(PEERS, 8, COLS)
        weights_ref[pl.ds(at, 8), :] = sums[COLS:]

    @pl.when(step == PAIRS // UNROLL - 1)
    def _():
        out_ref[:, COLS:, :] = weights_ref[...].T.reshape(PEERS, 8, COLS)


HIST_COST = pl.CostEstimate(
    flops=2 * ROW_DEV * HALF * BINS * 256, bytes_accessed=8 << 20, transcendentals=0
)


def own_sums(rows):
    return pl.pallas_call(
        own_kernel,
        grid=(PAIRS // UNROLL,),
        in_specs=[pl.BlockSpec(rows.shape, lambda i: (0, 0))],
        out_specs=pl.BlockSpec((UNROLL, SENT, LANES), lambda i: (i, 0, 0)),
        out_shape=jax.ShapeDtypeStruct((PAIRS, SENT, LANES), F32),
        scratch_shapes=[
            pltpu.VMEM((ROW_DEV, LANES), BF16),
            pltpu.VMEM((COLS + TARGETS, ROW_DEV), BF16),
        ],
        compiler_params=params(),
        cost_estimate=HIST_COST,
    )(rows)


def both_sums(rows, sums):
    return pl.pallas_call(
        both_kernel,
        grid=(PAIRS // UNROLL,),
        in_specs=[
            pl.BlockSpec(rows.shape, lambda i: (0, 0)),
            pl.BlockSpec((UNROLL, SENT, LANES), lambda i: (i, 0, 0)),
        ],
        out_specs=pl.BlockSpec((PEERS, SENT, COLS), lambda i: (0, 0, 0)),
        out_shape=jax.ShapeDtypeStruct((PEERS, SENT, COLS), F32),
        scratch_shapes=[
            pltpu.VMEM((ROW_DEV, LANES), BF16),
            pltpu.VMEM((COLS + TARGETS, ROW_DEV), BF16),
            pltpu.VMEM((COLS, LANES), F32),
        ],
        compiler_params=params(),
        cost_estimate=HIST_COST,
    )(rows, sums)


def place_kernel(bin_ref, aux_ref, column_ref, out_ref):
    aux = aux_ref[...].astype(F32)
    grads, weights, leaf = (aux[:TARGETS], aux[TARGETS : TARGETS + 1], aux[TARGETS + 1 : TARGETS + 2])
    child = jnp.where(column_ref[0:1, :] > bin_ref[0].astype(F32), 1.0, 0.0)
    key = leaf * 2 + child
    keys = 2 * LEAVES
    hot = jnp.where(iota((keys, ROW_DEV), 0).astype(F32) == key, 1.0, 0.0)
    width = 256
    earlier = jnp.where(iota((width, width), 0) < iota((width, width), 1), 1.0, 0.0).astype(BF16)
    counts = jnp.zeros((keys, 1), F32)
    ranks = []
    for i in range(ROW_DEV // width):
        part = hot[:, i * width : (i + 1) * width]
        before = jnp.dot(part.astype(BF16), earlier, preferred_element_type=F32) + counts
        ranks.append(jnp.sum(part * before, axis=0, keepdims=True))
        counts = counts + jnp.sum(part, axis=1, keepdims=True)
    rank = jnp.concatenate(ranks, axis=1)
    sibling = iota((keys, ROW_DEV), 0).astype(F32) == leaf * 2
    first = jnp.sum(jnp.where(sibling, counts, 0.0), axis=0, keepdims=True)
    slot = (leaf * CAP + rank + child * first).astype(I32)
    dims = (((1,), (1,)), ((), ()))
    group = 128 // TARGETS
    tiled = jnp.concatenate([grads] * group, axis=0)
    own = iota((128, ROW_DEV), 0) // TARGETS == slot % group
    values = jnp.where(own, tiled, 0.0).astype(BF16)
    line = iota((CAP // group, ROW_DEV), 0)
    for l in range(LEAVES):
        pick = jnp.where(line + l * (CAP // group) == slot // group, 1.0, 0.0).astype(BF16)
        moved = lax.dot_general(pick, values, dims, preferred_element_type=F32)
        out_ref[l, :COLS, :] = moved.astype(BF16)
    lane_values = jnp.where(iota((128, ROW_DEV), 0) == slot % 128, weights, 0.0).astype(BF16)
    pick = jnp.where(iota((LEAVES * CAP // 128, ROW_DEV), 0) == slot // 128, 1.0, 0.0).astype(BF16)
    moved = lax.dot_general(pick, lane_values, dims, preferred_element_type=F32)
    for l in range(LEAVES):
        part = jnp.concatenate([moved[l * 8 : (l + 1) * 8], jnp.zeros((8, 128), F32)], axis=0)
        out_ref[l, COLS:, :] = part.astype(BF16)


def place_rows(split_bin, aux, column):
    return pl.pallas_call(
        place_kernel,
        in_specs=[
            pl.BlockSpec(memory_space=pltpu.SMEM),
            pl.BlockSpec(aux.shape, lambda: (0, 0)),
            pl.BlockSpec(column.shape, lambda: (0, 0)),
        ],
        out_specs=pl.BlockSpec((LEAVES, COLS + 16, 128), lambda: (0, 0, 0)),
        out_shape=jax.ShapeDtypeStruct((LEAVES, COLS + 16, 128), BF16),
        compiler_params=params(),
        cost_estimate=pl.CostEstimate(
            flops=2 * LEAVES * CAP * ROW_DEV * 32, bytes_accessed=1 << 20, transcendentals=0
        ),
    )(split_bin, aux, column)


def gain_kernel(parts_ref, out_ref):
    total = lax.fori_loop(
        1, PEERS, lambda i, so_far: so_far + parts_ref[i], parts_ref[0], unroll=4
    )
    expand = jnp.where(
        iota((COLS, PAIRS * COLS), 0) == iota((COLS, PAIRS * COLS), 1) // TARGETS, 1.0, 0.0
    )
    spread_w = jnp.dot(
        total[COLS:], expand, preferred_element_type=F32, precision=lax.Precision.HIGHEST
    )
    grads = [total[i * 8 : (i + 1) * 8] for i in range(PAIRS)]
    weights = [spread_w[:, i * COLS : (i + 1) * COLS] for i in range(PAIRS)]
    row = iota((8, COLS), 0)
    even = row < OWNED

    def sides(values):
        swapped = [pltpu.roll(v, OWNED, 0) for v in values]
        both = [v + s for v, s in zip(values, swapped)]
        left, right = ([], [])
        below = jnp.zeros((8, COLS), F32)
        for v, b in zip(values, both):
            left.append(below + jnp.where(even, v, b))
            below = below + b
        above = jnp.zeros((8, COLS), F32)
        for s, b in zip(reversed(swapped), reversed(both)):
            right.append(above + jnp.where(even, s, 0.0))
            above = above + b
        return (left, right[::-1])

    left_g, right_g = sides(grads)
    left_w, right_w = sides(weights)
    place = lax.rem(row, OWNED) * BINS + row // OWNED
    gains = jnp.zeros((8, COLS), F32)
    for i in range(PAIRS):
        x, y = (left_w[i] + 1.0, right_w[i] + 1.0)
        diff = left_g[i] * y - right_g[i] * x
        terms = diff * diff / (x * y * (x + y))
        sums = jnp.sum(terms, axis=1, keepdims=True)
        gains = gains + jnp.where(iota((8, COLS), 1) == place + 2 * i, sums, 0.0)
    out_ref[...] = jnp.sum(gains, axis=0, keepdims=True) / (LEAVES * TARGETS)


def owned_gains(parts):
    return pl.pallas_call(
        gain_kernel,
        out_shape=jax.ShapeDtypeStruct((1, OWNED * BINS), F32),
        in_specs=[pl.BlockSpec(parts.shape, lambda: (0, 0, 0))],
        out_specs=pl.BlockSpec((1, OWNED * BINS), lambda: (0, 0)),
        compiler_params=params(),
    )(parts)


def exchange(blocks, axis):
    return lax.all_to_all(blocks, axis, split_axis=0, concat_axis=0, tiled=True)


def shards(bin_codes, leaf_index, gradients, row_weights, split_feature, split_bin):
    core = lax.axis_index("grp_1").astype(I32).reshape(1)
    aux = jnp.concatenate(
        [
            gradients.T,
            row_weights[None, :],
            leaf_index.reshape(1, ROW_DEV).astype(BF16),
            jnp.zeros((AUX - TARGETS - 2, ROW_DEV), BF16),
        ],
        axis=0,
    )
    own, send, column = prep(core, split_feature, bin_codes, aux)
    other = lax.ppermute(send, "grp_1", [(0, 1), (1, 0)])
    sums = both_sums(other, own_sums(own))
    arrived = exchange(sums, CHIPS)
    moved = exchange(place_rows(split_bin, aux, column), GRP)
    gains = owned_gains(arrived)
    everyone = exchange(jnp.broadcast_to(gains[None], (128, 1, OWNED * BINS)), ROWS_GRP)
    group = lax.axis_index(ROWS)
    table = lax.dynamic_slice_in_dim(everyone, group * 8, 8, 0).reshape(-1)
    best = jnp.max(everyone).reshape(1)
    moved_gradients = moved[:, :COLS].reshape(1, -1)
    moved_weights = moved[:, COLS : COLS + 8].reshape(1, -1)
    return (table, best, moved_gradients, moved_weights)


def solution(mesh):
    torus = Mesh(mesh.devices.reshape(4, 4, 4, 2), ("rows_0", "rows_1", "grp_0", "grp_1"))
    in_specs = (P(ROWS_GRP, None), P(ROWS_GRP, None), P(ROWS_GRP, None), P(ROWS_GRP), P(), P())
    out_specs = (P(ROWS), P(), P(ROWS_GRP, None), P(ROWS_GRP, None))
    return jax.shard_map(
        shards, mesh=torus, in_specs=in_specs, out_specs=out_specs, check_vma=False
    )
```

```python
import jax
import jax.numpy as jnp
from jax import lax
from jax.experimental import pallas as pl
from jax.experimental.pallas import tpu as pltpu
from jax.sharding import Mesh
from jax.sharding import PartitionSpec as P

BINS = 32
TARGETS = 16
LEAVES = 8
CAP = 1024
COLS = LEAVES * TARGETS
FEATURES = 512
HALF = FEATURES // 2
ROW_DEV = 4096
ROW_BLOCK = 512
PEERS = 64
OWNED = 4
PAIRS = BINS // 2
AUX = 32
AUX_CHUNK = HALF
AUX_ROWS = ROW_DEV // AUX_CHUNK * AUX
LANES = 2 * HALF
SENT = COLS + LEAVES
GRP = ("grp_0", "grp_1")
ROWS_GRP = ("rows_0", "rows_1", "grp_0", "grp_1")
ROWS = ("rows_0", "rows_1")
CHIPS = ("rows_0", "rows_1", "grp_0")
F32 = jnp.float32
BF16 = jnp.bfloat16
I32 = jnp.int32


def iota(shape, dim):
    return lax.broadcasted_iota(I32, shape, dim)


def params(mib):
    return pltpu.CompilerParams(vmem_limit_bytes=mib << 20)


def prep_kernel(
    core_ref, feature_ref, codes_ref, grads_ref, weights_ref, leaf_ref, own_ref, send_ref, column_ref, aux_ref, select_ref
):
    step = pl.program_id(0)
    blocks = ROW_DEV // ROW_BLOCK

    @pl.when(step == 0)
    def _():
        core = core_ref[0]
        lane = iota((1, FEATURES), 1)
        side = jnp.where(lane < HALF, core, 1 - core)
        place = lane & (HALF - 1)
        wanted = ((place >> 2) << 3) + (side << 2) + (place & 3)
        select_ref[...] = jnp.where(iota((FEATURES, FEATURES), 0) == wanted, 1.0, 0.0).astype(BF16)

    @pl.when(step < blocks)
    def _():
        codes = codes_ref[...].astype(F32).astype(BF16)
        both = jnp.dot(codes, select_ref[...], preferred_element_type=F32).astype(BF16)
        own_ref[...] = both[:, :HALF]
        send_ref[...] = both[:, HALF:]
        hot = jnp.where(iota((8, FEATURES), 1) == feature_ref[0], 1.0, 0.0).astype(BF16)
        column_ref[...] = lax.dot_general(
            hot, codes, (((1,), (1,)), ((), ())), preferred_element_type=F32
        )

    @pl.when(step == blocks)
    def _():
        weights = weights_ref[...].astype(F32)
        leaf = leaf_ref[...].astype(F32)
        row = iota((TARGETS, AUX_CHUNK), 0)
        for i in range(ROW_DEV // AUX_CHUNK):
            lanes = slice(i * AUX_CHUNK, (i + 1) * AUX_CHUNK)
            weight = jnp.concatenate([weights[2 * i : 2 * i + 1], weights[2 * i + 1 : 2 * i + 2]], axis=1)
            rest = jnp.where(row == 0, weight, jnp.where(row == 1, leaf[:, lanes], 0.0)).astype(BF16)
            for ref in (own_ref, send_ref, aux_ref):
                ref[i * AUX : i * AUX + TARGETS, :] = grads_ref[:, lanes]
                ref[i * AUX + TARGETS : (i + 1) * AUX, :] = rest


def prep(core, split_feature, codes, grads, weights, leaf):
    blocks = ROW_DEV // ROW_BLOCK
    smem = pl.BlockSpec(memory_space=pltpu.SMEM)
    buffer = jax.ShapeDtypeStruct((ROW_DEV + AUX_ROWS, HALF), BF16)
    return pl.pallas_call(
        prep_kernel,
        grid=(blocks + 1,),
        in_specs=[
            smem,
            smem,
            pl.BlockSpec((ROW_BLOCK, FEATURES), lambda i: (jnp.minimum(i, blocks - 1), 0)),
            pl.BlockSpec(grads.shape, lambda i: (0, 0)),
            pl.BlockSpec(weights.shape, lambda i: (0, 0)),
            pl.BlockSpec(leaf.shape, lambda i: (0, 0)),
        ],
        out_specs=[
            pl.BlockSpec((ROW_BLOCK, HALF), lambda i: (i, 0)),
            pl.BlockSpec((ROW_BLOCK, HALF), lambda i: (i, 0)),
            pl.BlockSpec((8, ROW_BLOCK), lambda i: (0, jnp.minimum(i, blocks - 1))),
            pl.BlockSpec((AUX_ROWS, HALF), lambda i: (0, 0)),
        ],
        out_shape=[
            buffer,
            buffer,
            jax.ShapeDtypeStruct((8, ROW_DEV), F32),
            jax.ShapeDtypeStruct((AUX_ROWS, HALF), BF16),
        ],
        scratch_shapes=[pltpu.VMEM((FEATURES, FEATURES), BF16)],
        compiler_params=params(56),
        cost_estimate=pl.CostEstimate(
            flops=2 * ROW_DEV * FEATURES * FEATURES,
            bytes_accessed=ROW_DEV * FEATURES * 6,
            transcendentals=0,
        ),
    )(core, split_feature, codes, grads, weights, leaf)


def unpack_aux(rows_ref, at):
    parts = [
        rows_ref[at + i * AUX : at + (i + 1) * AUX, :]
        for i in range(ROW_DEV // AUX_CHUNK)
    ]
    return jnp.concatenate(parts, axis=1).astype(F32)


def spread(rows_ref, dup_ref, data_ref):
    lane = iota((1, LANES), 1)
    source = ((lane >> 3) << 2) + (lane & 3)
    twice = jnp.where(iota((HALF, LANES), 0) == source, 1.0, 0.0).astype(BF16)
    for i in range(ROW_DEV // ROW_BLOCK):
        rows = slice(i * ROW_BLOCK, (i + 1) * ROW_BLOCK)
        dup_ref[rows, :] = jnp.dot(
            rows_ref[rows, :], twice, preferred_element_type=F32
        ).astype(BF16)
    aux = unpack_aux(rows_ref, ROW_DEV)
    grads, weights, leaf = (aux[:TARGETS], aux[TARGETS : TARGETS + 1], aux[TARGETS + 1 : TARGETS + 2])
    for l in range(LEAVES):
        data_ref[l * TARGETS : (l + 1) * TARGETS, :] = jnp.where(leaf == l, grads, 0.0).astype(BF16)
    ids = iota((TARGETS, ROW_DEV), 0).astype(F32)
    data_ref[COLS : COLS + TARGETS, :] = jnp.where(leaf == ids, weights, 0.0).astype(BF16)


def pair_sums(pair, dup_ref, data_ref):
    lane = iota((1, LANES), 1)
    wanted = (2 * pair + ((lane >> 2) & 1)).astype(F32).astype(BF16)
    hot = jnp.where(dup_ref[...] == wanted, jnp.ones((), BF16), jnp.zeros((), BF16))
    return jnp.dot(data_ref[...], hot, preferred_element_type=F32)[:SENT]


UNROLL = 4
BITS = 15.0
MESSAGE = COLS + 16


def own_kernel(rows_ref, sums_ref, dup_ref, data_ref):
    step = pl.program_id(0)

    @pl.when(step == 0)
    def _():
        spread(rows_ref, dup_ref, data_ref)

    for i in range(UNROLL):
        sums_ref[i] = pair_sums(step * UNROLL + i, dup_ref, data_ref)


def both_kernel(rows_ref, sums_ref, out_ref, dup_ref, data_ref, total_ref, largest_ref, weights_ref):
    step = pl.program_id(0)

    @pl.when(step == 0)
    def _():
        spread(rows_ref, dup_ref, data_ref)
        largest_ref[...] = jnp.zeros(largest_ref.shape, F32)

    for i in range(UNROLL):
        pair = step * UNROLL + i
        sums = pair_sums(pair, dup_ref, data_ref) + sums_ref[i]
        at = pl.multiple_of(pair * 8, 8)
        turned = sums[:COLS].T.reshape(PEERS, 8, COLS)
        total_ref[:, pl.ds(at, 8), :] = turned
        largest_ref[...] = jnp.maximum(largest_ref[...], jnp.abs(turned))
        weights_ref[pl.ds(at, 8), :] = sums[COLS:]

    @pl.when(step == PAIRS // UNROLL - 1)
    def _():
        weights = weights_ref[...].T.reshape(PEERS, 8, COLS)
        most = jnp.abs(weights)
        for lanes in (8, 16, 32, 64):
            most = jnp.maximum(most, pltpu.roll(most, lanes, 2))
        exp_g, exp_w = (exponents(largest_ref[...]), exponents(most))
        scale_g, scale_w = (jnp.exp2(BITS - exp_g), jnp.exp2(BITS - exp_w))
        for i in range(COLS // 16):
            rows = slice(i * 16, (i + 1) * 16)
            twice = jnp.concatenate([scale_g, scale_g], axis=1)
            out_ref[:, rows, :] = whole(total_ref[:, rows, :] * twice)
        even = iota((PEERS, 8, COLS), 1) < OWNED
        last = [weights * scale_w, jnp.where(even, exp_g, exp_w)]
        out_ref[:, COLS:, :] = whole(jnp.concatenate(last, axis=1))


def exponents(magnitudes):
    most = jnp.maximum(magnitudes, pltpu.roll(magnitudes, OWNED, 1))
    return jnp.ceil(jnp.log2(jnp.maximum(most, 1e-30)) + 0.001)


def whole(values):
    return jnp.round(values).astype(I32).astype(jnp.int16)


HIST_COST = pl.CostEstimate(
    flops=2 * ROW_DEV * HALF * BINS * 256, bytes_accessed=8 << 20, transcendentals=0
)


def own_sums(rows):
    return pl.pallas_call(
        own_kernel,
        grid=(PAIRS // UNROLL,),
        in_specs=[pl.BlockSpec(rows.shape, lambda i: (0, 0))],
        out_specs=pl.BlockSpec((UNROLL, SENT, LANES), lambda i: (i, 0, 0)),
        out_shape=jax.ShapeDtypeStruct((PAIRS, SENT, LANES), F32),
        scratch_shapes=[
            pltpu.VMEM((ROW_DEV, LANES), BF16),
            pltpu.VMEM((COLS + TARGETS, ROW_DEV), BF16),
        ],
        compiler_params=params(36),
        cost_estimate=HIST_COST,
    )(rows)


def both_sums(rows, sums):
    return pl.pallas_call(
        both_kernel,
        grid=(PAIRS // UNROLL,),
        in_specs=[
            pl.BlockSpec(rows.shape, lambda i: (0, 0)),
            pl.BlockSpec((UNROLL, SENT, LANES), lambda i: (i, 0, 0)),
        ],
        out_specs=pl.BlockSpec((PEERS, MESSAGE, COLS), lambda i: (0, 0, 0)),
        out_shape=pltpu.HBM((PEERS, MESSAGE, COLS), jnp.int16),
        scratch_shapes=[
            pltpu.VMEM((ROW_DEV, LANES), BF16),
            pltpu.VMEM((COLS + TARGETS, ROW_DEV), BF16),
            pltpu.VMEM((PEERS, COLS, COLS), F32),
            pltpu.VMEM((PEERS, 8, COLS), F32),
            pltpu.VMEM((COLS, LANES), F32),
        ],
        compiler_params=params(40),
        cost_estimate=HIST_COST,
    )(rows, sums)


def place_kernel(core_ref, bin_ref, aux_ref, column_ref, keep_ref, give_ref):
    core = core_ref[0]
    aux = unpack_aux(aux_ref, 0)
    grads, weights, leaf = (aux[:TARGETS], aux[TARGETS : TARGETS + 1], aux[TARGETS + 1 : TARGETS + 2])
    child = jnp.where(column_ref[0:1, :] > bin_ref[0].astype(F32), 1.0, 0.0)
    key = leaf * 2 + child
    keys = 2 * LEAVES
    hot = jnp.where(iota((keys, ROW_DEV), 0).astype(F32) == key, 1.0, 0.0)
    width = 256
    earlier = jnp.where(iota((width, width), 0) < iota((width, width), 1), 1.0, 0.0).astype(BF16)
    counts = jnp.zeros((keys, 1), F32)
    ranks = []
    for i in range(ROW_DEV // width):
        part = hot[:, i * width : (i + 1) * width]
        before = jnp.dot(part.astype(BF16), earlier, preferred_element_type=F32) + counts
        ranks.append(jnp.sum(part * before, axis=0, keepdims=True))
        counts = counts + jnp.sum(part, axis=1, keepdims=True)
    rank = jnp.concatenate(ranks, axis=1)
    sibling = iota((keys, ROW_DEV), 0).astype(F32) == leaf * 2
    first = jnp.sum(jnp.where(sibling, counts, 0.0), axis=0, keepdims=True)
    slot = (leaf * CAP + rank + child * first).astype(I32)
    dims = (((1,), (1,)), ((), ()))
    group = 128 // TARGETS
    tiled = jnp.concatenate([grads] * group, axis=0)
    values = jnp.where(iota((128, 1), 0) >> 4 == (slot & (group - 1)), tiled, 0.0).astype(BF16)
    lines = CAP // group
    line = iota((lines, 1), 0)
    for l in range(LEAVES):
        target = 2 * (l % 4) + (core if l < 4 else 1 - core)
        out_ref = keep_ref if l < 4 else give_ref
        pick = jnp.where(line == (slot >> 3) - target * lines, 1.0, 0.0).astype(BF16)
        moved = lax.dot_general(pick, values, dims, preferred_element_type=F32)
        out_ref[l % 4, :COLS, :] = moved.astype(BF16)
    lane_values = jnp.where(iota((128, 1), 0) == (slot & 127), weights, 0.0).astype(BF16)
    blocks = CAP // 128
    for l in range(LEAVES):
        target = 2 * (l % 4) + (core if l < 4 else 1 - core)
        out_ref = keep_ref if l < 4 else give_ref
        pick = jnp.where(iota((16, 1), 0) == (slot >> 7) - target * blocks, 1.0, 0.0)
        pick = jnp.where(iota((16, 1), 0) < blocks, pick, 0.0).astype(BF16)
        moved = lax.dot_general(pick, lane_values, dims, preferred_element_type=F32)
        out_ref[l % 4, COLS:, :] = moved.astype(BF16)


def place_rows(core, split_bin, aux, column):
    smem = pl.BlockSpec(memory_space=pltpu.SMEM)
    block = jax.ShapeDtypeStruct((LEAVES // 2, COLS + 16, 128), BF16)
    spec = pl.BlockSpec(block.shape, lambda i: (0, 0, 0))
    return pl.pallas_call(
        place_kernel,
        grid=(1,),
        in_specs=[
            smem,
            smem,
            pl.BlockSpec(aux.shape, lambda i: (0, 0)),
            pl.BlockSpec(column.shape, lambda i: (0, 0)),
        ],
        out_specs=[spec, spec],
        out_shape=[block, block],
        compiler_params=params(24),
        cost_estimate=pl.CostEstimate(
            flops=2 * LEAVES * CAP * ROW_DEV * 32, bytes_accessed=1 << 20, transcendentals=0
        ),
    )(core, split_bin, aux, column)


def deliver(keep, give):
    core, chip = (lax.axis_index("grp_1"), lax.axis_index("grp_0"))
    got = lax.ppermute(give, "grp_1", [(0, 1), (1, 0)])
    first = jnp.where(core == 0, keep, got)
    second = jnp.where(core == 0, got, keep)
    blocks = jnp.stack([first, second], axis=1)
    arrived = []
    for s in range(4):
        block = lax.dynamic_index_in_dim(blocks, (chip + s) % 4, 0, keepdims=False)
        if s:
            block = lax.ppermute(block, "grp_0", [(i, (i + s) % 4) for i in range(4)])
        arrived.append(block)
    turned = jnp.stack([arrived[0], arrived[3], arrived[2], arrived[1]] * 2)
    ordered = lax.dynamic_slice_in_dim(turned, (4 - chip) % 4, 4, 0)
    return ordered.reshape(8, COLS + 16, 128)


def gain_kernel(parts_ref, out_ref):
    upper = iota((8, COLS), 0) < OWNED

    def add_part(p, so_far):
        tail = parts_ref[p, COLS:, :].astype(I32).astype(F32)
        powers = jnp.exp2(tail[8:] - BITS)
        turned = pltpu.roll(powers, OWNED, 0)
        scale_g = jnp.where(upper, powers, turned)
        scale_w = jnp.where(upper, turned, powers)
        values = parts_ref[p, :COLS, :].astype(I32).astype(F32)
        added = [so_far[i] + values[i * 8 : (i + 1) * 8] * scale_g for i in range(PAIRS)]
        return (*added, so_far[PAIRS] + tail[:8] * scale_w)

    start = tuple(jnp.zeros((8, COLS), F32) for _ in range(PAIRS + 1))
    total = lax.fori_loop(0, PEERS, add_part, start, unroll=4)
    expand = jnp.where(
        iota((COLS, 1), 0) == iota((1, PAIRS * COLS), 1) >> 4, 1.0, 0.0
    )
    spread_w = jnp.dot(
        total[PAIRS], expand, preferred_element_type=F32, precision=lax.Precision.HIGHEST
    )
    grads = total[:PAIRS]
    weights = [spread_w[:, i * COLS : (i + 1) * COLS] for i in range(PAIRS)]
    row = iota((8, COLS), 0)
    even = row < OWNED

    def sides(values):
        swapped = [pltpu.roll(v, OWNED, 0) for v in values]
        both = [v + s for v, s in zip(values, swapped)]
        left, right = ([], [])
        below = jnp.zeros((8, COLS), F32)
        for v, b in zip(values, both):
            left.append(below + jnp.where(even, v, b))
            below = below + b
        above = jnp.zeros((8, COLS), F32)
        for s, b in zip(reversed(swapped), reversed(both)):
            right.append(above + jnp.where(even, s, 0.0))
            above = above + b
        return (left, right[::-1])

    left_g, right_g = sides(grads)
    left_w, right_w = sides(weights)
    place = (row & (OWNED - 1)) * BINS + (row >> 2)
    gains = jnp.zeros((8, COLS), F32)
    for i in range(PAIRS):
        x, y = (left_w[i] + 1.0, right_w[i] + 1.0)
        diff = left_g[i] * y - right_g[i] * x
        terms = diff * diff / (x * y * (x + y))
        sums = jnp.sum(terms, axis=1, keepdims=True)
        gains = gains + jnp.where(iota((8, COLS), 1) == place + 2 * i, sums, 0.0)
    gains = jnp.sum(gains, axis=0, keepdims=True) / (LEAVES * TARGETS)
    out_ref[...] = jnp.broadcast_to(gains[None], out_ref.shape)


def owned_gains(parts):
    shape = (2 * PEERS, 1, OWNED * BINS)
    return pl.pallas_call(
        gain_kernel,
        out_shape=jax.ShapeDtypeStruct(shape, F32),
        in_specs=[pl.BlockSpec(parts.shape, lambda: (0, 0, 0))],
        out_specs=pl.BlockSpec(shape, lambda: (0, 0, 0)),
        compiler_params=params(16),
    )(parts)


def close_kernel(group_ref, gains_ref, table_ref, best_ref):
    table_ref[...] = gains_ref[pl.ds(group_ref[0] * 8, 8)]
    highest = jnp.max(gains_ref[...], axis=0)
    best_ref[...] = jnp.max(highest, axis=1, keepdims=True)


def close(group, gains):
    return pl.pallas_call(
        close_kernel,
        out_shape=[
            jax.ShapeDtypeStruct((8, 1, OWNED * BINS), F32),
            jax.ShapeDtypeStruct((1, 1), F32),
        ],
        in_specs=[
            pl.BlockSpec(memory_space=pltpu.SMEM),
            pl.BlockSpec(gains.shape, lambda: (0, 0, 0)),
        ],
        out_specs=[
            pl.BlockSpec((8, 1, OWNED * BINS), lambda: (0, 0, 0)),
            pl.BlockSpec((1, 1), lambda: (0, 0)),
        ],
        compiler_params=params(4),
    )(group, gains)


def exchange(blocks, axis):
    return lax.all_to_all(blocks, axis, split_axis=0, concat_axis=0, tiled=True)


def shards(bin_codes, leaf_index, gradients, row_weights, split_feature, split_bin):
    core = lax.axis_index("grp_1").astype(I32).reshape(1)
    own, send, column, aux = prep(
        core,
        split_feature,
        bin_codes,
        gradients.T,
        row_weights.reshape(ROW_DEV // 128, 128),
        leaf_index.reshape(1, ROW_DEV),
    )
    other = lax.ppermute(send, "grp_1", [(0, 1), (1, 0)])
    sums = both_sums(other, own_sums(own))
    arrived = exchange(sums, CHIPS)
    aux, column, unused = lax.optimization_barrier((aux, column, sums))
    moved = deliver(*place_rows(core, split_bin, aux, column))
    everyone = exchange(owned_gains(arrived), ROWS_GRP)
    table, best = close(lax.axis_index(ROWS).astype(I32).reshape(1), everyone)
    table, best = (table.reshape(-1), best.reshape(1))
    moved_gradients = moved[:, :COLS].reshape(1, -1)
    moved_weights = moved[:, COLS : COLS + 8].reshape(1, -1)
    return (table, best, moved_gradients, moved_weights)


def solution(mesh):
    torus = Mesh(mesh.devices.reshape(4, 4, 4, 2), ("rows_0", "rows_1", "grp_0", "grp_1"))
    in_specs = (P(ROWS_GRP, None), P(ROWS_GRP, None), P(ROWS_GRP, None), P(ROWS_GRP), P(), P())
    out_specs = (P(ROWS), P(), P(ROWS_GRP, None), P(ROWS_GRP, None))
    return jax.shard_map(
        shards, mesh=torus, in_specs=in_specs, out_specs=out_specs, check_vma=False
    )
```

```python
import jax
import jax.numpy as jnp
from jax import lax
from jax.experimental import pallas as pl
from jax.experimental.pallas import tpu as pltpu
from jax.sharding import Mesh
from jax.sharding import PartitionSpec as P

BINS = 32
TARGETS = 16
LEAVES = 8
CAP = 1024
COLS = LEAVES * TARGETS
FEATURES = 512
HALF = FEATURES // 2
ROW_DEV = 4096
ROW_BLOCK = 512
PEERS = 64
OWNED = 4
PAIRS = BINS // 2
AUX = 32
AUX_CHUNK = HALF
AUX_ROWS = ROW_DEV // AUX_CHUNK * AUX
LANES = 2 * HALF
SENT = COLS + LEAVES
GRP = ("grp_0", "grp_1")
ROWS_GRP = ("rows_0", "rows_1", "grp_0", "grp_1")
ROWS = ("rows_0", "rows_1")
CHIPS = ("rows_0", "rows_1", "grp_0")
F32 = jnp.float32
BF16 = jnp.bfloat16
I32 = jnp.int32


def iota(shape, dim):
    return lax.broadcasted_iota(I32, shape, dim)


def in_hbm(array):
    return pltpu.with_memory_space_constraint(array, pltpu.HBM)


def params(mib):
    return pltpu.CompilerParams(vmem_limit_bytes=mib << 20)


def prep_kernel(
    core_ref, codes_hbm, grads_hbm, weights_hbm, leaf_hbm, dup_hbm, send_hbm, data_hbm, aux_hbm,
    codes_ref, grads_ref, weights_ref, leaf_ref, dup_ref, send_ref, data_ref, aux_ref, in_sems, out_sems,
):
    blocks = ROW_DEV // ROW_BLOCK
    cuts = [slice(i * ROW_BLOCK, (i + 1) * ROW_BLOCK) for i in range(blocks)]
    pairs = [(grads_hbm, grads_ref), (weights_hbm, weights_ref), (leaf_hbm, leaf_ref)]
    pairs += [(codes_hbm.at[rows, :], codes_ref.at[rows, :]) for rows in cuts]
    arriving = [pltpu.make_async_copy(a, b, in_sems.at[i]) for i, (a, b) in enumerate(pairs)]
    for copy in arriving:
        copy.start()
    leaving = []

    def leave(source, target):
        copy = pltpu.make_async_copy(source, target, out_sems.at[len(leaving)])
        copy.start()
        leaving.append(copy)

    core = core_ref[0]
    lane = iota((1, LANES + HALF), 1)
    twice = ((lane >> 3) << 3) + (core << 2) + (lane & 3)
    place = lane - LANES
    once = ((place >> 2) << 3) + ((1 - core) << 2) + (place & 3)
    wanted = jnp.where(lane < LANES, twice, once)
    select = jnp.where(iota((FEATURES, LANES + HALF), 0) == wanted, 1.0, 0.0).astype(BF16)

    for copy in arriving[:3]:
        copy.wait()
    weights = weights_ref[...].astype(F32)
    row = iota((TARGETS, ROW_DEV), 0)
    weight = jnp.concatenate([weights[i : i + 1] for i in range(weights.shape[0])], axis=1)
    leaf = leaf_ref[...].astype(F32)
    rest = jnp.where(row == 0, weight, jnp.where(row == 1, leaf, 0.0)).astype(BF16)
    aux_ref[:TARGETS, :] = grads_ref[...]
    aux_ref[TARGETS:, :] = rest
    leave(aux_ref, aux_hbm)
    for i in range(ROW_DEV // AUX_CHUNK):
        lanes = slice(i * AUX_CHUNK, (i + 1) * AUX_CHUNK)
        at = ROW_DEV + i * AUX
        send_ref[at : at + TARGETS, :] = grads_ref[:, lanes]
        send_ref[at + TARGETS : at + AUX, :] = rest[:, lanes]
    leave(send_ref.at[ROW_DEV:, :], send_hbm.at[ROW_DEV:, :])
    spread_values(grads_ref[...].astype(F32), weight, leaf, data_ref)
    leave(data_ref, data_hbm)

    for rows, copy in zip(cuts, arriving[3:]):
        copy.wait()
        codes = codes_ref[rows, :].astype(F32).astype(BF16)
        both = jnp.dot(codes, select, preferred_element_type=F32).astype(BF16)
        dup_ref[rows, :] = both[:, :LANES]
        send_ref[rows, :] = both[:, LANES:]
        leave(dup_ref.at[rows, :], dup_hbm.at[rows, :])
        leave(send_ref.at[rows, :], send_hbm.at[rows, :])
    for copy in leaving:
        copy.wait()


def spread_values(grads, weights, leaf, data_ref):
    for l in range(LEAVES):
        data_ref[l * TARGETS : (l + 1) * TARGETS, :] = jnp.where(leaf == l, grads, 0.0).astype(BF16)
    ids = iota((TARGETS, ROW_DEV), 0).astype(F32)
    data_ref[COLS : COLS + TARGETS, :] = jnp.where(leaf == ids, weights, 0.0).astype(BF16)


def prep(core, codes, grads, weights, leaf):
    blocks = ROW_DEV // ROW_BLOCK
    there = pl.BlockSpec(memory_space=pl.ANY)
    outs = [
        (ROW_DEV, LANES),
        (ROW_DEV + AUX_ROWS, HALF),
        (COLS + TARGETS, ROW_DEV),
        (AUX, ROW_DEV),
    ]
    ins = [codes, grads, weights, leaf]
    return pl.pallas_call(
        prep_kernel,
        in_specs=[pl.BlockSpec(memory_space=pltpu.SMEM)] + [there] * len(ins),
        out_specs=[there] * len(outs),
        out_shape=[pltpu.HBM(shape, BF16) for shape in outs],
        scratch_shapes=[pltpu.VMEM(a.shape, a.dtype) for a in ins]
        + [pltpu.VMEM(shape, BF16) for shape in outs]
        + [pltpu.SemaphoreType.DMA((blocks + 3,)), pltpu.SemaphoreType.DMA((2 * blocks + 3,))],
        compiler_params=params(48),
        cost_estimate=pl.CostEstimate(
            flops=2 * ROW_DEV * FEATURES * FEATURES,
            bytes_accessed=ROW_DEV * FEATURES * 8,
            transcendentals=0,
        ),
    )(core, *[in_hbm(a) for a in ins])


def split_aux(aux):
    return (aux[:TARGETS], aux[TARGETS : TARGETS + 1], aux[TARGETS + 1 : TARGETS + 2])


def spread(rows_ref, dup_ref, data_ref):
    lane = iota((1, LANES), 1)
    source = ((lane >> 3) << 2) + (lane & 3)
    twice = jnp.where(iota((HALF, LANES), 0) == source, 1.0, 0.0).astype(BF16)
    for i in range(ROW_DEV // ROW_BLOCK):
        rows = slice(i * ROW_BLOCK, (i + 1) * ROW_BLOCK)
        dup_ref[rows, :] = jnp.dot(
            rows_ref[rows, :], twice, preferred_element_type=F32
        ).astype(BF16)
    parts = [
        rows_ref[ROW_DEV + i * AUX : ROW_DEV + (i + 1) * AUX, :]
        for i in range(ROW_DEV // AUX_CHUNK)
    ]
    aux = jnp.concatenate(parts, axis=1).astype(F32)
    spread_values(*split_aux(aux), data_ref)


def pair_sums(pair, dup_ref, data_ref):
    lane = iota((1, LANES), 1)
    wanted = (2 * pair + ((lane >> 2) & 1)).astype(F32).astype(BF16)
    hot = jnp.where(dup_ref[...] == wanted, jnp.ones((), BF16), jnp.zeros((), BF16))
    return jnp.dot(data_ref[...], hot, preferred_element_type=F32)[:SENT]


UNROLL = 4
BITS = 15.0
MESSAGE = COLS + 16


def own_kernel(dup_ref, data_ref, sums_ref):
    step = pl.program_id(0)
    for i in range(UNROLL):
        sums_ref[i] = pair_sums(step * UNROLL + i, dup_ref, data_ref)


def both_kernel(rows_ref, sums_ref, out_ref, dup_ref, data_ref, total_ref, largest_ref, weights_ref):
    step = pl.program_id(0)

    @pl.when(step == 0)
    def _():
        spread(rows_ref, dup_ref, data_ref)
        largest_ref[...] = jnp.zeros(largest_ref.shape, F32)

    for i in range(UNROLL):
        pair = step * UNROLL + i
        sums = pair_sums(pair, dup_ref, data_ref) + sums_ref[i]
        at = pl.multiple_of(pair * 8, 8)
        turned = sums[:COLS].T.reshape(PEERS, 8, COLS)
        total_ref[:, pl.ds(at, 8), :] = turned
        largest_ref[...] = jnp.maximum(largest_ref[...], jnp.abs(turned))
        weights_ref[pl.ds(at, 8), :] = sums[COLS:]

    @pl.when(step == PAIRS // UNROLL - 1)
    def _():
        weights = weights_ref[...].T.reshape(PEERS, 8, COLS)
        most = jnp.abs(weights)
        for lanes in (8, 16, 32, 64):
            most = jnp.maximum(most, pltpu.roll(most, lanes, 2))
        exp_g, exp_w = (exponents(largest_ref[...]), exponents(most))
        scale_g, scale_w = (jnp.exp2(BITS - exp_g), jnp.exp2(BITS - exp_w))
        for i in range(COLS // 16):
            rows = slice(i * 16, (i + 1) * 16)
            twice = jnp.concatenate([scale_g, scale_g], axis=1)
            out_ref[:, rows, :] = whole(total_ref[:, rows, :] * twice)
        even = iota((PEERS, 8, COLS), 1) < OWNED
        last = [weights * scale_w, jnp.where(even, exp_g, exp_w)]
        out_ref[:, COLS:, :] = whole(jnp.concatenate(last, axis=1))


def exponents(magnitudes):
    most = jnp.maximum(magnitudes, pltpu.roll(magnitudes, OWNED, 1))
    return jnp.ceil(jnp.log2(jnp.maximum(most, 1e-30)) + 0.001)


def whole(values):
    return jnp.round(values).astype(I32).astype(jnp.int16)


HIST_COST = pl.CostEstimate(
    flops=2 * ROW_DEV * HALF * BINS * 256, bytes_accessed=8 << 20, transcendentals=0
)


def own_sums(dup, data):
    still = pl.Buffered(1)
    return pl.pallas_call(
        own_kernel,
        grid=(PAIRS // UNROLL,),
        in_specs=[
            pl.BlockSpec(dup.shape, lambda i: (0, 0), pipeline_mode=still),
            pl.BlockSpec(data.shape, lambda i: (0, 0), pipeline_mode=still),
        ],
        out_specs=pl.BlockSpec((UNROLL, SENT, LANES), lambda i: (i, 0, 0)),
        out_shape=jax.ShapeDtypeStruct((PAIRS, SENT, LANES), F32),
        compiler_params=params(36),
        cost_estimate=HIST_COST,
    )(in_hbm(dup), in_hbm(data))


def both_sums(rows, sums):
    return pl.pallas_call(
        both_kernel,
        grid=(PAIRS // UNROLL,),
        in_specs=[
            pl.BlockSpec(rows.shape, lambda i: (0, 0)),
            pl.BlockSpec((UNROLL, SENT, LANES), lambda i: (i, 0, 0)),
        ],
        out_specs=pl.BlockSpec((PEERS, MESSAGE, COLS), lambda i: (0, 0, 0)),
        out_shape=pltpu.HBM((PEERS, MESSAGE, COLS), jnp.int16),
        scratch_shapes=[
            pltpu.VMEM((ROW_DEV, LANES), BF16),
            pltpu.VMEM((COLS + TARGETS, ROW_DEV), BF16),
            pltpu.VMEM((PEERS, COLS, COLS), F32),
            pltpu.VMEM((PEERS, 8, COLS), F32),
            pltpu.VMEM((COLS, LANES), F32),
        ],
        compiler_params=params(40),
        cost_estimate=HIST_COST,
    )(rows, sums)


def place_kernel(feature_ref, core_ref, bin_ref, aux_ref, codes_ref, keep_ref, give_ref):
    core = core_ref[0]
    grads, weights, leaf = split_aux(aux_ref[...].astype(F32))
    chosen = jnp.where(iota((8, 128), 1) == (feature_ref[0] & 127), 1.0, 0.0).astype(BF16)
    column = lax.dot_general(
        chosen,
        codes_ref[...].astype(F32).astype(BF16),
        (((1,), (1,)), ((), ())),
        preferred_element_type=F32,
    )[0:1]
    child = jnp.where(column > bin_ref[0].astype(F32), 1.0, 0.0)
    key = leaf * 2 + child
    keys = 2 * LEAVES
    hot = jnp.where(iota((keys, ROW_DEV), 0).astype(F32) == key, 1.0, 0.0)
    width = 256
    earlier = jnp.where(iota((width, width), 0) < iota((width, width), 1), 1.0, 0.0).astype(BF16)
    counts = jnp.zeros((keys, 1), F32)
    ranks = []
    for i in range(ROW_DEV // width):
        part = hot[:, i * width : (i + 1) * width]
        before = jnp.dot(part.astype(BF16), earlier, preferred_element_type=F32) + counts
        ranks.append(jnp.sum(part * before, axis=0, keepdims=True))
        counts = counts + jnp.sum(part, axis=1, keepdims=True)
    rank = jnp.concatenate(ranks, axis=1)
    sibling = iota((keys, ROW_DEV), 0).astype(F32) == leaf * 2
    first = jnp.sum(jnp.where(sibling, counts, 0.0), axis=0, keepdims=True)
    slot = (leaf * CAP + rank + child * first).astype(I32)
    dims = (((1,), (1,)), ((), ()))
    group = 128 // TARGETS
    tiled = jnp.concatenate([grads] * group, axis=0)
    values = jnp.where(iota((128, 1), 0) >> 4 == (slot & (group - 1)), tiled, 0.0).astype(BF16)
    lines = CAP // group
    line = iota((lines, 1), 0)
    for l in range(LEAVES):
        target = 2 * (l % 4) + (core if l < 4 else 1 - core)
        out_ref = keep_ref if l < 4 else give_ref
        pick = jnp.where(line == (slot >> 3) - target * lines, 1.0, 0.0).astype(BF16)
        moved = lax.dot_general(pick, values, dims, preferred_element_type=F32)
        out_ref[l % 4, :COLS, :] = moved.astype(BF16)
    lane_values = jnp.where(iota((128, 1), 0) == (slot & 127), weights, 0.0).astype(BF16)
    blocks = CAP // 128
    for l in range(LEAVES):
        target = 2 * (l % 4) + (core if l < 4 else 1 - core)
        out_ref = keep_ref if l < 4 else give_ref
        pick = jnp.where(iota((16, 1), 0) == (slot >> 7) - target * blocks, 1.0, 0.0)
        pick = jnp.where(iota((16, 1), 0) < blocks, pick, 0.0).astype(BF16)
        moved = lax.dot_general(pick, lane_values, dims, preferred_element_type=F32)
        out_ref[l % 4, COLS:, :] = moved.astype(BF16)


def place_rows(split_feature, core, split_bin, aux, codes):
    smem = pl.BlockSpec(memory_space=pltpu.SMEM)
    block = jax.ShapeDtypeStruct((LEAVES // 2, COLS + 16, 128), BF16)
    spec = pl.BlockSpec(block.shape, lambda i, feature: (0, 0, 0))
    return pl.pallas_call(
        place_kernel,
        grid_spec=pltpu.PrefetchScalarGridSpec(
            num_scalar_prefetch=1,
            grid=(1,),
            in_specs=[
                smem,
                smem,
                pl.BlockSpec(aux.shape, lambda i, feature: (0, 0)),
                pl.BlockSpec((ROW_DEV, 128), lambda i, feature: (0, feature[0] >> 7)),
            ],
            out_specs=[spec, spec],
        ),
        out_shape=[block, block],
        compiler_params=params(56),
        cost_estimate=pl.CostEstimate(
            flops=2 * LEAVES * CAP * ROW_DEV * 32, bytes_accessed=1 << 20, transcendentals=0
        ),
    )(split_feature, core, split_bin, aux, codes)


def deliver(keep, give):
    core, chip = (lax.axis_index("grp_1"), lax.axis_index("grp_0"))
    got = lax.ppermute(give, "grp_1", [(0, 1), (1, 0)])
    first = jnp.where(core == 0, keep, got)
    second = jnp.where(core == 0, got, keep)
    blocks = jnp.stack([first, second], axis=1)
    arrived = []
    for s in range(4):
        block = lax.dynamic_index_in_dim(blocks, (chip + s) % 4, 0, keepdims=False)
        if s:
            block = lax.ppermute(block, "grp_0", [(i, (i + s) % 4) for i in range(4)])
        arrived.append(block)
    turned = jnp.stack([arrived[0], arrived[3], arrived[2], arrived[1]] * 2)
    ordered = lax.dynamic_slice_in_dim(turned, (4 - chip) % 4, 4, 0)
    return ordered.reshape(8, COLS + 16, 128)


def gain_kernel(parts_ref, out_ref):
    upper = iota((8, COLS), 0) < OWNED

    def add_part(p, so_far):
        tail = parts_ref[p, COLS:, :].astype(I32).astype(F32)
        powers = jnp.exp2(tail[8:] - BITS)
        turned = pltpu.roll(powers, OWNED, 0)
        scale_g = jnp.where(upper, powers, turned)
        scale_w = jnp.where(upper, turned, powers)
        values = parts_ref[p, :COLS, :].astype(I32).astype(F32)
        added = [so_far[i] + values[i * 8 : (i + 1) * 8] * scale_g for i in range(PAIRS)]
        return (*added, so_far[PAIRS] + tail[:8] * scale_w)

    start = tuple(jnp.zeros((8, COLS), F32) for _ in range(PAIRS + 1))
    total = lax.fori_loop(0, PEERS, add_part, start, unroll=4)
    expand = jnp.where(
        iota((COLS, 1), 0) == iota((1, PAIRS * COLS), 1) >> 4, 1.0, 0.0
    )
    spread_w = jnp.dot(
        total[PAIRS], expand, preferred_element_type=F32, precision=lax.Precision.HIGHEST
    )
    grads = total[:PAIRS]
    weights = [spread_w[:, i * COLS : (i + 1) * COLS] for i in range(PAIRS)]
    row = iota((8, COLS), 0)
    even = row < OWNED

    def sides(values):
        swapped = [pltpu.roll(v, OWNED, 0) for v in values]
        both = [v + s for v, s in zip(values, swapped)]
        left, right = ([], [])
        below = jnp.zeros((8, COLS), F32)
        for v, b in zip(values, both):
            left.append(below + jnp.where(even, v, b))
            below = below + b
        above = jnp.zeros((8, COLS), F32)
        for s, b in zip(reversed(swapped), reversed(both)):
            right.append(above + jnp.where(even, s, 0.0))
            above = above + b
        return (left, right[::-1])

    left_g, right_g = sides(grads)
    left_w, right_w = sides(weights)
    place = (row & (OWNED - 1)) * BINS + (row >> 2)
    gains = jnp.zeros((8, COLS), F32)
    for i in range(PAIRS):
        x, y = (left_w[i] + 1.0, right_w[i] + 1.0)
        diff = left_g[i] * y - right_g[i] * x
        terms = diff * diff / (x * y * (x + y))
        sums = jnp.sum(terms, axis=1, keepdims=True)
        gains = gains + jnp.where(iota((8, COLS), 1) == place + 2 * i, sums, 0.0)
    gains = jnp.sum(gains, axis=0, keepdims=True) / (LEAVES * TARGETS)
    out_ref[...] = jnp.broadcast_to(gains[None], out_ref.shape)


def owned_gains(parts):
    shape = (2 * PEERS, 1, OWNED * BINS)
    return pl.pallas_call(
        gain_kernel,
        out_shape=jax.ShapeDtypeStruct(shape, F32),
        in_specs=[pl.BlockSpec(parts.shape, lambda: (0, 0, 0))],
        out_specs=pl.BlockSpec(shape, lambda: (0, 0, 0)),
        compiler_params=params(16),
    )(parts)


def close_kernel(group_ref, gains_ref, table_ref, best_ref):
    table_ref[...] = gains_ref[pl.ds(group_ref[0] * 8, 8)]
    highest = jnp.max(gains_ref[...], axis=0)
    best_ref[...] = jnp.max(highest, axis=1, keepdims=True)


def close(group, gains):
    return pl.pallas_call(
        close_kernel,
        out_shape=[
            jax.ShapeDtypeStruct((8, 1, OWNED * BINS), F32),
            jax.ShapeDtypeStruct((1, 1), F32),
        ],
        in_specs=[
            pl.BlockSpec(memory_space=pltpu.SMEM),
            pl.BlockSpec(gains.shape, lambda: (0, 0, 0)),
        ],
        out_specs=[
            pl.BlockSpec((8, 1, OWNED * BINS), lambda: (0, 0, 0)),
            pl.BlockSpec((1, 1), lambda: (0, 0)),
        ],
        compiler_params=params(4),
    )(group, gains)


def exchange(blocks, axis):
    return lax.all_to_all(blocks, axis, split_axis=0, concat_axis=0, tiled=True)


def shards(bin_codes, leaf_index, gradients, row_weights, split_feature, split_bin):
    core = lax.axis_index("grp_1").astype(I32).reshape(1)
    dup, send, data, aux = prep(
        core,
        bin_codes,
        gradients.T,
        row_weights.reshape(ROW_DEV // 128, 128),
        leaf_index.reshape(1, ROW_DEV),
    )
    other = lax.ppermute(send, "grp_1", [(0, 1), (1, 0)])
    sums = both_sums(other, own_sums(dup, data))
    arrived = exchange(sums, CHIPS)
    aux, unused = lax.optimization_barrier((aux, sums))
    moved = deliver(*place_rows(split_feature, core, split_bin, aux, bin_codes))
    everyone = exchange(owned_gains(arrived), ROWS_GRP)
    table, best = close(lax.axis_index(ROWS).astype(I32).reshape(1), everyone)
    table, best = (table.reshape(-1), best.reshape(1))
    moved_gradients = moved[:, :COLS].reshape(1, -1)
    moved_weights = moved[:, COLS : COLS + 8].reshape(1, -1)
    return (table, best, moved_gradients, moved_weights)


def solution(mesh):
    torus = Mesh(mesh.devices.reshape(4, 4, 4, 2), ("rows_0", "rows_1", "grp_0", "grp_1"))
    in_specs = (P(ROWS_GRP, None), P(ROWS_GRP, None), P(ROWS_GRP, None), P(ROWS_GRP), P(), P())
    out_specs = (P(ROWS), P(), P(ROWS_GRP, None), P(ROWS_GRP, None))
    return jax.shard_map(
        shards, mesh=torus, in_specs=in_specs, out_specs=out_specs, check_vma=False
    )
```

```python
import jax
import jax.numpy as jnp
from jax import lax
from jax.experimental import pallas as pl
from jax.experimental.pallas import tpu as pltpu
from jax.sharding import Mesh
from jax.sharding import PartitionSpec as P

BINS = 32
TARGETS = 16
LEAVES = 8
CAP = 1024
COLS = LEAVES * TARGETS
FEATURES = 512
HALF = FEATURES // 2
ROW_DEV = 4096
ROW_BLOCK = 512
PEERS = 64
OWNED = 4
PAIRS = BINS // 2
AUX = 32
AUX_CHUNK = HALF
AUX_ROWS = ROW_DEV // AUX_CHUNK * AUX
SENT = COLS + LEAVES
GRP = ("grp_0", "grp_1")
ROWS_GRP = ("rows_0", "rows_1", "grp_0", "grp_1")
ROWS = ("rows_0", "rows_1")
CHIPS = ("rows_0", "rows_1", "grp_0")
F32 = jnp.float32
BF16 = jnp.bfloat16
I32 = jnp.int32


def iota(shape, dim):
    return lax.broadcasted_iota(I32, shape, dim)


def in_hbm(array):
    return pltpu.with_memory_space_constraint(array, pltpu.HBM)


def params(mib):
    return pltpu.CompilerParams(vmem_limit_bytes=mib << 20)


def value_rows(weights, leaf):
    lines = weights.astype(F32)
    weight = jnp.concatenate([lines[i : i + 1] for i in range(lines.shape[0])], axis=1)
    return (weight, leaf.astype(F32))


def prep_kernel(
    core_ref, codes_hbm, grads_hbm, weights_hbm, leaf_hbm, send_hbm, aux_hbm,
    codes_ref, grads_ref, weights_ref, leaf_ref, send_ref, aux_ref, in_sems, out_sems,
):
    cuts = row_cuts()
    theirs = pl.ds(pl.multiple_of((1 - core_ref[0]) * HALF, HALF), HALF)
    pairs = [(grads_hbm, grads_ref), (weights_hbm, weights_ref), (leaf_hbm, leaf_ref)]
    pairs += [(codes_hbm.at[rows, theirs], codes_ref.at[rows, :]) for rows in cuts]
    arriving = [pltpu.make_async_copy(a, b, in_sems.at[i]) for i, (a, b) in enumerate(pairs)]
    for copy in arriving:
        copy.start()
    leaving = []

    def leave(source, target):
        copy = pltpu.make_async_copy(source, target, out_sems.at[len(leaving)])
        copy.start()
        leaving.append(copy)

    for copy in arriving[:3]:
        copy.wait()
    weight, leaf = value_rows(weights_ref[...], leaf_ref[...])
    row = iota((TARGETS, ROW_DEV), 0)
    rest = jnp.where(row == 0, weight, jnp.where(row == 1, leaf, 0.0)).astype(BF16)
    aux_ref[:TARGETS, :] = grads_ref[...]
    aux_ref[TARGETS:, :] = rest
    leave(aux_ref, aux_hbm)
    for i in range(ROW_DEV // AUX_CHUNK):
        lanes = slice(i * AUX_CHUNK, (i + 1) * AUX_CHUNK)
        at = ROW_DEV + i * AUX
        send_ref[at : at + TARGETS, :] = grads_ref[:, lanes]
        send_ref[at + TARGETS : at + AUX, :] = rest[:, lanes]
    leave(send_ref.at[ROW_DEV:, :], send_hbm.at[ROW_DEV:, :])
    for rows, copy in zip(cuts, arriving[3:]):
        copy.wait()
        send_ref[rows, :] = codes_ref[rows, :].astype(F32).astype(BF16)
        leave(send_ref.at[rows, :], send_hbm.at[rows, :])
    for copy in leaving:
        copy.wait()


def row_cuts():
    return [slice(i * ROW_BLOCK, (i + 1) * ROW_BLOCK) for i in range(ROW_DEV // ROW_BLOCK)]


def spread_values(grads, weights, leaf, data_ref):
    for l in range(LEAVES):
        data_ref[l * TARGETS : (l + 1) * TARGETS, :] = jnp.where(leaf == l, grads, 0.0).astype(BF16)
    ids = iota((TARGETS, ROW_DEV), 0).astype(F32)
    data_ref[COLS : COLS + TARGETS, :] = jnp.where(leaf == ids, weights, 0.0).astype(BF16)


def prep(core, codes, grads, weights, leaf):
    blocks = ROW_DEV // ROW_BLOCK
    there = pl.BlockSpec(memory_space=pl.ANY)
    outs = [(ROW_DEV + AUX_ROWS, HALF), (AUX, ROW_DEV)]
    ins = [codes, grads, weights, leaf]
    return pl.pallas_call(
        prep_kernel,
        in_specs=[pl.BlockSpec(memory_space=pltpu.SMEM)] + [there] * len(ins),
        out_specs=[there] * len(outs),
        out_shape=[pltpu.HBM(shape, BF16) for shape in outs],
        scratch_shapes=[pltpu.VMEM((ROW_DEV, HALF), I32)]
        + [pltpu.VMEM(a.shape, a.dtype) for a in ins[1:]]
        + [pltpu.VMEM(shape, BF16) for shape in outs]
        + [pltpu.SemaphoreType.DMA((blocks + 3,)), pltpu.SemaphoreType.DMA((blocks + 2,))],
        compiler_params=params(32),
        cost_estimate=pl.CostEstimate(
            flops=ROW_DEV * HALF, bytes_accessed=ROW_DEV * HALF * 6, transcendentals=0
        ),
    )(core, *[in_hbm(a) for a in ins])


def split_aux(aux):
    return (aux[:TARGETS], aux[TARGETS : TARGETS + 1], aux[TARGETS + 1 : TARGETS + 2])


def bin_sums(index, codes_ref, data_ref):
    wanted = jnp.full((1, HALF), 0.0, F32) + index.astype(F32)
    hot = jnp.where(codes_ref[...] == wanted.astype(BF16), jnp.ones((), BF16), jnp.zeros((), BF16))
    return jnp.dot(data_ref[...], hot, preferred_element_type=F32)[:SENT]


UNROLL = 4
BITS = 15.0
MESSAGE = COLS + 16


def own_kernel(
    core_ref, codes_hbm, grads_hbm, weights_hbm, leaf_hbm, sums_ref,
    whole_ref, grads_ref, weights_ref, leaf_ref, codes_ref, data_ref, sems,
):
    step = pl.program_id(0)

    @pl.when(step == 0)
    def _():
        ours = pl.ds(pl.multiple_of(core_ref[0] * HALF, HALF), HALF)
        pairs = [(grads_hbm, grads_ref), (weights_hbm, weights_ref), (leaf_hbm, leaf_ref)]
        pairs += [(codes_hbm.at[rows, ours], whole_ref.at[rows, :]) for rows in row_cuts()]
        arriving = [pltpu.make_async_copy(a, b, sems.at[i]) for i, (a, b) in enumerate(pairs)]
        for copy in arriving:
            copy.start()
        for copy in arriving[:3]:
            copy.wait()
        weight, leaf = value_rows(weights_ref[...], leaf_ref[...])
        spread_values(grads_ref[...].astype(F32), weight, leaf, data_ref)
        for rows, copy in zip(row_cuts(), arriving[3:]):
            copy.wait()
            codes_ref[rows, :] = whole_ref[rows, :].astype(F32).astype(BF16)

    for i in range(2 * UNROLL):
        sums_ref[i] = bin_sums(step * (2 * UNROLL) + i, codes_ref, data_ref)


def interleave(even, odd):
    even, odd = (v.T.reshape(PEERS // 2, 8, COLS) for v in (even, odd))
    low = iota(even.shape, 1) < OWNED
    first = jnp.where(low, even, pltpu.roll(odd, OWNED, 1))
    second = jnp.where(low, pltpu.roll(even, OWNED, 1), odd)
    return (first, second)


def both_kernel(rows_ref, sums_ref, out_ref, data_ref, total_ref, largest_ref, even_ref, odd_ref):
    step = pl.program_id(0)

    @pl.when(step == 0)
    def _():
        parts = [
            rows_ref[ROW_DEV + i * AUX : ROW_DEV + (i + 1) * AUX, :]
            for i in range(ROW_DEV // AUX_CHUNK)
        ]
        aux = jnp.concatenate(parts, axis=1).astype(F32)
        spread_values(*split_aux(aux), data_ref)
        largest_ref[...] = jnp.zeros(largest_ref.shape, F32)

    codes_ref = rows_ref.at[:ROW_DEV, :]
    for i in range(UNROLL):
        pair = step * UNROLL + i
        even = bin_sums(2 * pair, codes_ref, data_ref) + sums_ref[2 * i]
        odd = bin_sums(2 * pair + 1, codes_ref, data_ref) + sums_ref[2 * i + 1]
        at = pl.multiple_of(pair * 8, 8)
        for side, values in enumerate(interleave(even[:COLS], odd[:COLS])):
            total_ref[:, side, pl.ds(at, 8), :] = values
            largest_ref[:, side] = jnp.maximum(largest_ref[:, side], jnp.abs(values))
        even_ref[pl.ds(at, 8), :] = even[COLS:]
        odd_ref[pl.ds(at, 8), :] = odd[COLS:]

    @pl.when(step == PAIRS // UNROLL - 1)
    def _():
        low = iota((PEERS // 2, 8, COLS), 1) < OWNED
        for side, weights in enumerate(interleave(even_ref[...], odd_ref[...])):
            most = jnp.abs(weights)
            for lanes in (8, 16, 32, 64):
                most = jnp.maximum(most, pltpu.roll(most, lanes, 2))
            exp_g, exp_w = (exponents(largest_ref[:, side]), exponents(most))
            scale_g, scale_w = (jnp.exp2(BITS - exp_g), jnp.exp2(BITS - exp_w))
            twice = jnp.concatenate([scale_g, scale_g], axis=1)
            for i in range(COLS // 16):
                rows = slice(i * 16, (i + 1) * 16)
                out_ref[:, side, rows, :] = whole(total_ref[:, side, rows, :] * twice)
            last = [weights * scale_w, jnp.where(low, exp_g, exp_w)]
            out_ref[:, side, COLS:, :] = whole(jnp.concatenate(last, axis=1))


def exponents(magnitudes):
    most = jnp.maximum(magnitudes, pltpu.roll(magnitudes, OWNED, 1))
    return jnp.ceil(jnp.log2(jnp.maximum(most, 1e-30)) + 0.001)


def whole(values):
    return jnp.round(values).astype(I32).astype(jnp.int16)


HIST_COST = pl.CostEstimate(
    flops=2 * ROW_DEV * HALF * BINS * 256, bytes_accessed=8 << 20, transcendentals=0
)


def own_sums(core, codes, grads, weights, leaf):
    ins = [codes, grads, weights, leaf]
    return pl.pallas_call(
        own_kernel,
        grid=(PAIRS // UNROLL,),
        in_specs=[pl.BlockSpec(memory_space=pltpu.SMEM)]
        + [pl.BlockSpec(memory_space=pl.ANY)] * len(ins),
        out_specs=pl.BlockSpec((2 * UNROLL, SENT, HALF), lambda i: (i, 0, 0)),
        out_shape=jax.ShapeDtypeStruct((BINS, SENT, HALF), F32),
        scratch_shapes=[pltpu.VMEM((ROW_DEV, HALF), I32)]
        + [pltpu.VMEM(a.shape, a.dtype) for a in ins[1:]]
        + [
            pltpu.VMEM((ROW_DEV, HALF), BF16),
            pltpu.VMEM((COLS + TARGETS, ROW_DEV), BF16),
            pltpu.SemaphoreType.DMA((ROW_DEV // ROW_BLOCK + 3,)),
        ],
        compiler_params=params(36),
        cost_estimate=HIST_COST,
    )(core, *[in_hbm(a) for a in ins])


def both_sums(rows, sums):
    halved = (PEERS // 2, 2)
    out = pl.pallas_call(
        both_kernel,
        grid=(PAIRS // UNROLL,),
        in_specs=[
            pl.BlockSpec(rows.shape, lambda i: (0, 0), pipeline_mode=pl.Buffered(1)),
            pl.BlockSpec((2 * UNROLL, SENT, HALF), lambda i: (i, 0, 0)),
        ],
        out_specs=pl.BlockSpec((*halved, MESSAGE, COLS), lambda i: (0, 0, 0, 0)),
        out_shape=pltpu.HBM((*halved, MESSAGE, COLS), jnp.int16),
        scratch_shapes=[
            pltpu.VMEM((COLS + TARGETS, ROW_DEV), BF16),
            pltpu.VMEM((*halved, COLS, COLS), F32),
            pltpu.VMEM((*halved, 8, COLS), F32),
            pltpu.VMEM((COLS, HALF), F32),
            pltpu.VMEM((COLS, HALF), F32),
        ],
        compiler_params=params(40),
        cost_estimate=HIST_COST,
    )(rows, sums)
    return out.reshape(PEERS, MESSAGE, COLS)


def place_kernel(feature_ref, core_ref, bin_ref, aux_ref, codes_ref, keep_ref, give_ref):
    core = core_ref[0]
    grads, weights, leaf = split_aux(aux_ref[...].astype(F32))
    chosen = jnp.where(iota((8, 128), 1) == (feature_ref[0] & 127), 1.0, 0.0).astype(BF16)
    column = lax.dot_general(
        chosen,
        codes_ref[...].astype(F32).astype(BF16),
        (((1,), (1,)), ((), ())),
        preferred_element_type=F32,
    )[0:1]
    child = jnp.where(column > bin_ref[0].astype(F32), 1.0, 0.0)
    key = leaf * 2 + child
    keys = 2 * LEAVES
    hot = jnp.where(iota((keys, ROW_DEV), 0).astype(F32) == key, 1.0, 0.0)
    width = 256
    earlier = jnp.where(iota((width, width), 0) < iota((width, width), 1), 1.0, 0.0).astype(BF16)
    counts = jnp.zeros((keys, 1), F32)
    ranks = []
    for i in range(ROW_DEV // width):
        part = hot[:, i * width : (i + 1) * width]
        before = jnp.dot(part.astype(BF16), earlier, preferred_element_type=F32) + counts
        ranks.append(jnp.sum(part * before, axis=0, keepdims=True))
        counts = counts + jnp.sum(part, axis=1, keepdims=True)
    rank = jnp.concatenate(ranks, axis=1)
    sibling = iota((keys, ROW_DEV), 0).astype(F32) == leaf * 2
    first = jnp.sum(jnp.where(sibling, counts, 0.0), axis=0, keepdims=True)
    slot = (leaf * CAP + rank + child * first).astype(I32)
    dims = (((1,), (1,)), ((), ()))
    group = 128 // TARGETS
    tiled = jnp.concatenate([grads] * group, axis=0)
    values = jnp.where(iota((128, 1), 0) >> 4 == (slot & (group - 1)), tiled, 0.0).astype(BF16)
    lines = CAP // group
    line = iota((lines, 1), 0)
    for l in range(LEAVES):
        target = 2 * (l % 4) + (core if l < 4 else 1 - core)
        out_ref = keep_ref if l < 4 else give_ref
        pick = jnp.where(line == (slot >> 3) - target * lines, 1.0, 0.0).astype(BF16)
        moved = lax.dot_general(pick, values, dims, preferred_element_type=F32)
        out_ref[l % 4, :COLS, :] = moved.astype(BF16)
    lane_values = jnp.where(iota((128, 1), 0) == (slot & 127), weights, 0.0).astype(BF16)
    blocks = CAP // 128
    for l in range(LEAVES):
        target = 2 * (l % 4) + (core if l < 4 else 1 - core)
        out_ref = keep_ref if l < 4 else give_ref
        pick = jnp.where(iota((16, 1), 0) == (slot >> 7) - target * blocks, 1.0, 0.0)
        pick = jnp.where(iota((16, 1), 0) < blocks, pick, 0.0).astype(BF16)
        moved = lax.dot_general(pick, lane_values, dims, preferred_element_type=F32)
        out_ref[l % 4, COLS:, :] = moved.astype(BF16)


def place_rows(split_feature, core, split_bin, aux, codes):
    smem = pl.BlockSpec(memory_space=pltpu.SMEM)
    block = jax.ShapeDtypeStruct((LEAVES // 2, COLS + 16, 128), BF16)
    spec = pl.BlockSpec(block.shape, lambda i, feature: (0, 0, 0))
    return pl.pallas_call(
        place_kernel,
        grid_spec=pltpu.PrefetchScalarGridSpec(
            num_scalar_prefetch=1,
            grid=(1,),
            in_specs=[
                smem,
                smem,
                pl.BlockSpec(aux.shape, lambda i, feature: (0, 0)),
                pl.BlockSpec((ROW_DEV, 128), lambda i, feature: (0, feature[0] >> 7)),
            ],
            out_specs=[spec, spec],
        ),
        out_shape=[block, block],
        compiler_params=params(56),
        cost_estimate=pl.CostEstimate(
            flops=2 * LEAVES * CAP * ROW_DEV * 32, bytes_accessed=1 << 20, transcendentals=0
        ),
    )(split_feature, core, split_bin, aux, codes)


def deliver(keep, give):
    core, chip = (lax.axis_index("grp_1"), lax.axis_index("grp_0"))
    got = lax.ppermute(give, "grp_1", [(0, 1), (1, 0)])
    first = jnp.where(core == 0, keep, got)
    second = jnp.where(core == 0, got, keep)
    blocks = jnp.stack([first, second], axis=1)
    arrived = []
    for s in range(4):
        block = lax.dynamic_index_in_dim(blocks, (chip + s) % 4, 0, keepdims=False)
        if s:
            block = lax.ppermute(block, "grp_0", [(i, (i + s) % 4) for i in range(4)])
        arrived.append(block)
    turned = jnp.stack([arrived[0], arrived[3], arrived[2], arrived[1]] * 2)
    ordered = lax.dynamic_slice_in_dim(turned, (4 - chip) % 4, 4, 0)
    return ordered.reshape(8, COLS + 16, 128)


def gain_kernel(parts_ref, out_ref):
    upper = iota((8, COLS), 0) < OWNED

    def add_part(p, so_far):
        tail = parts_ref[p, COLS:, :].astype(I32).astype(F32)
        powers = jnp.exp2(tail[8:] - BITS)
        turned = pltpu.roll(powers, OWNED, 0)
        scale_g = jnp.where(upper, powers, turned)
        scale_w = jnp.where(upper, turned, powers)
        values = parts_ref[p, :COLS, :].astype(I32).astype(F32)
        added = [so_far[i] + values[i * 8 : (i + 1) * 8] * scale_g for i in range(PAIRS)]
        return (*added, so_far[PAIRS] + tail[:8] * scale_w)

    start = tuple(jnp.zeros((8, COLS), F32) for _ in range(PAIRS + 1))
    total = lax.fori_loop(0, PEERS, add_part, start, unroll=4)
    expand = jnp.where(
        iota((COLS, 1), 0) == iota((1, PAIRS * COLS), 1) >> 4, 1.0, 0.0
    )
    spread_w = jnp.dot(
        total[PAIRS], expand, preferred_element_type=F32, precision=lax.Precision.HIGHEST
    )
    grads = total[:PAIRS]
    weights = [spread_w[:, i * COLS : (i + 1) * COLS] for i in range(PAIRS)]
    row = iota((8, COLS), 0)
    even = row < OWNED

    def sides(values):
        swapped = [pltpu.roll(v, OWNED, 0) for v in values]
        both = [v + s for v, s in zip(values, swapped)]
        left, right = ([], [])
        below = jnp.zeros((8, COLS), F32)
        for v, b in zip(values, both):
            left.append(below + jnp.where(even, v, b))
            below = below + b
        above = jnp.zeros((8, COLS), F32)
        for s, b in zip(reversed(swapped), reversed(both)):
            right.append(above + jnp.where(even, s, 0.0))
            above = above + b
        return (left, right[::-1])

    left_g, right_g = sides(grads)
    left_w, right_w = sides(weights)
    place = (row & (OWNED - 1)) * BINS + (row >> 2)
    gains = jnp.zeros((8, COLS), F32)
    for i in range(PAIRS):
        x, y = (left_w[i] + 1.0, right_w[i] + 1.0)
        diff = left_g[i] * y - right_g[i] * x
        terms = diff * diff / (x * y * (x + y))
        sums = jnp.sum(terms, axis=1, keepdims=True)
        gains = gains + jnp.where(iota((8, COLS), 1) == place + 2 * i, sums, 0.0)
    gains = jnp.sum(gains, axis=0, keepdims=True) / (LEAVES * TARGETS)
    out_ref[...] = jnp.broadcast_to(gains[None], out_ref.shape)


def owned_gains(parts):
    shape = (2 * PEERS, 1, OWNED * BINS)
    return pl.pallas_call(
        gain_kernel,
        out_shape=jax.ShapeDtypeStruct(shape, F32),
        in_specs=[pl.BlockSpec(parts.shape, lambda: (0, 0, 0))],
        out_specs=pl.BlockSpec(shape, lambda: (0, 0, 0)),
        compiler_params=params(16),
    )(parts)


def close_kernel(group_ref, gains_ref, table_ref, best_ref):
    group = group_ref[0]
    first = (group & 7) * 16 + (group >> 3)
    for i in range(8):
        table_ref[i] = gains_ref[first + 2 * i]
    highest = jnp.max(gains_ref[...], axis=0)
    best_ref[...] = jnp.max(highest, axis=1, keepdims=True)


def close(group, gains):
    return pl.pallas_call(
        close_kernel,
        out_shape=[
            jax.ShapeDtypeStruct((8, 1, OWNED * BINS), F32),
            jax.ShapeDtypeStruct((1, 1), F32),
        ],
        in_specs=[
            pl.BlockSpec(memory_space=pltpu.SMEM),
            pl.BlockSpec(gains.shape, lambda: (0, 0, 0)),
        ],
        out_specs=[
            pl.BlockSpec((8, 1, OWNED * BINS), lambda: (0, 0, 0)),
            pl.BlockSpec((1, 1), lambda: (0, 0)),
        ],
        compiler_params=params(4),
    )(group, gains)


def exchange(blocks, axis):
    return lax.all_to_all(blocks, axis, split_axis=0, concat_axis=0, tiled=True)


def shards(bin_codes, leaf_index, gradients, row_weights, split_feature, split_bin):
    core = lax.axis_index("grp_1").astype(I32).reshape(1)
    values = (gradients.T, row_weights.reshape(ROW_DEV // 128, 128), leaf_index.reshape(1, ROW_DEV))
    send, aux = prep(core, bin_codes, *values)
    other = lax.ppermute(send, "grp_1", [(0, 1), (1, 0)])
    sums = both_sums(other, own_sums(core, bin_codes, *values))
    arrived = exchange(sums, CHIPS)
    aux, unused = lax.optimization_barrier((aux, sums))
    moved = deliver(*place_rows(split_feature, core, split_bin, aux, bin_codes))
    everyone = exchange(owned_gains(arrived), ROWS_GRP)
    table, best = close(lax.axis_index(ROWS).astype(I32).reshape(1), everyone)
    table, best = (table.reshape(-1), best.reshape(1))
    moved_gradients = moved[:, :COLS].reshape(1, -1)
    moved_weights = moved[:, COLS : COLS + 8].reshape(1, -1)
    return (table, best, moved_gradients, moved_weights)


def solution(mesh):
    torus = Mesh(mesh.devices.reshape(4, 4, 4, 2), ("rows_0", "rows_1", "grp_0", "grp_1"))
    in_specs = (P(ROWS_GRP, None), P(ROWS_GRP, None), P(ROWS_GRP, None), P(ROWS_GRP), P(), P())
    out_specs = (P(ROWS), P(), P(ROWS_GRP, None), P(ROWS_GRP, None))
    return jax.shard_map(
        shards, mesh=torus, in_specs=in_specs, out_specs=out_specs, check_vma=False
    )
```

```python
import jax
import jax.numpy as jnp
from jax import lax
from jax.experimental import pallas as pl
from jax.experimental.pallas import tpu as pltpu
from jax.sharding import Mesh
from jax.sharding import PartitionSpec as P

BINS = 32
TARGETS = 16
LEAVES = 8
CAP = 1024
COLS = LEAVES * TARGETS
FEATURES = 512
HALF = FEATURES // 2
ROW_DEV = 4096
ROW_BLOCK = 512
PEERS = 64
OWNED = 4
PAIRS = BINS // 2
AUX = 32
AUX_CHUNK = HALF
AUX_ROWS = ROW_DEV // AUX_CHUNK * AUX
SENT = COLS + LEAVES
GRP = ("grp_0", "grp_1")
ROWS_GRP = ("rows_0", "rows_1", "grp_0", "grp_1")
ROWS = ("rows_0", "rows_1")
CHIPS = ("rows_0", "rows_1", "grp_0")
F32 = jnp.float32
BF16 = jnp.bfloat16
I32 = jnp.int32


def iota(shape, dim):
    return lax.broadcasted_iota(I32, shape, dim)


def in_hbm(array):
    return pltpu.with_memory_space_constraint(array, pltpu.HBM)


def params(mib):
    return pltpu.CompilerParams(vmem_limit_bytes=mib << 20)


def value_rows(weights, leaf):
    lines = weights.astype(F32)
    weight = jnp.concatenate([lines[i : i + 1] for i in range(lines.shape[0])], axis=1)
    return (weight, leaf.astype(F32))


def prep_kernel(
    core_ref, codes_hbm, grads_hbm, weights_hbm, leaf_hbm, send_hbm, aux_hbm,
    codes_ref, grads_ref, weights_ref, leaf_ref, send_ref, aux_ref, in_sems, out_sems,
):
    cuts = row_cuts()
    theirs = pl.ds(pl.multiple_of((1 - core_ref[0]) * HALF, HALF), HALF)
    pairs = [(grads_hbm, grads_ref), (weights_hbm, weights_ref), (leaf_hbm, leaf_ref)]
    pairs += [(codes_hbm.at[rows, theirs], codes_ref.at[rows, :]) for rows in cuts]
    arriving = [pltpu.make_async_copy(a, b, in_sems.at[i]) for i, (a, b) in enumerate(pairs)]
    for copy in arriving:
        copy.start()
    leaving = []

    def leave(source, target):
        copy = pltpu.make_async_copy(source, target, out_sems.at[len(leaving)])
        copy.start()
        leaving.append(copy)

    for copy in arriving[:3]:
        copy.wait()
    weight, leaf = value_rows(weights_ref[...], leaf_ref[...])
    row = iota((TARGETS, ROW_DEV), 0)
    rest = jnp.where(row == 0, weight, jnp.where(row == 1, leaf, 0.0)).astype(BF16)
    aux_ref[:TARGETS, :] = grads_ref[...]
    aux_ref[TARGETS:, :] = rest
    leave(aux_ref, aux_hbm)
    for i in range(ROW_DEV // AUX_CHUNK):
        lanes = slice(i * AUX_CHUNK, (i + 1) * AUX_CHUNK)
        at = ROW_DEV + i * AUX
        send_ref[at : at + TARGETS, :] = grads_ref[:, lanes]
        send_ref[at + TARGETS : at + AUX, :] = rest[:, lanes]
    leave(send_ref.at[ROW_DEV:, :], send_hbm.at[ROW_DEV:, :])
    for rows, copy in zip(cuts, arriving[3:]):
        copy.wait()
        send_ref[rows, :] = codes_ref[rows, :].astype(F32).astype(BF16)
        leave(send_ref.at[rows, :], send_hbm.at[rows, :])
    for copy in leaving:
        copy.wait()


def row_cuts():
    return [slice(i * ROW_BLOCK, (i + 1) * ROW_BLOCK) for i in range(ROW_DEV // ROW_BLOCK)]


def spread_values(grads, weights, leaf, data_ref):
    for l in range(LEAVES):
        data_ref[l * TARGETS : (l + 1) * TARGETS, :] = jnp.where(leaf == l, grads, 0.0).astype(BF16)
    ids = iota((TARGETS, ROW_DEV), 0).astype(F32)
    data_ref[COLS : COLS + TARGETS, :] = jnp.where(leaf == ids, weights, 0.0).astype(BF16)


def prep(core, codes, grads, weights, leaf):
    blocks = ROW_DEV // ROW_BLOCK
    there = pl.BlockSpec(memory_space=pl.ANY)
    outs = [(ROW_DEV + AUX_ROWS, HALF), (AUX, ROW_DEV)]
    ins = [codes, grads, weights, leaf]
    return pl.pallas_call(
        prep_kernel,
        in_specs=[pl.BlockSpec(memory_space=pltpu.SMEM)] + [there] * len(ins),
        out_specs=[there] * len(outs),
        out_shape=[pltpu.HBM(shape, BF16) for shape in outs],
        scratch_shapes=[pltpu.VMEM((ROW_DEV, HALF), I32)]
        + [pltpu.VMEM(a.shape, a.dtype) for a in ins[1:]]
        + [pltpu.VMEM(shape, BF16) for shape in outs]
        + [pltpu.SemaphoreType.DMA((blocks + 3,)), pltpu.SemaphoreType.DMA((blocks + 2,))],
        compiler_params=params(32),
        cost_estimate=pl.CostEstimate(
            flops=ROW_DEV * HALF, bytes_accessed=ROW_DEV * HALF * 6, transcendentals=0
        ),
    )(core, *[in_hbm(a) for a in ins])


def split_aux(aux):
    return (aux[:TARGETS], aux[TARGETS : TARGETS + 1], aux[TARGETS + 1 : TARGETS + 2])


def bin_sums(index, codes_ref, data_ref, rows=slice(None)):
    wanted = jnp.full((1, HALF), 0.0, F32) + index.astype(F32)
    codes = codes_ref[rows, :]
    hot = jnp.where(codes == wanted.astype(BF16), jnp.ones((), BF16), jnp.zeros((), BF16))
    return jnp.dot(data_ref[:, rows], hot, preferred_element_type=F32)[:SENT]


ROW_HALVES = (slice(0, ROW_DEV // 2), slice(ROW_DEV // 2, ROW_DEV))


UNROLL = 4
DEEPER = 8
BITS = 15.0
MESSAGE = COLS + 16


def own_kernel(
    core_ref, codes_hbm, grads_hbm, weights_hbm, leaf_hbm, sums_ref,
    whole_ref, grads_ref, weights_ref, leaf_ref, codes_ref, data_ref, sems,
):
    step = pl.program_id(0)

    @pl.when(step == 0)
    def _():
        ours = pl.ds(pl.multiple_of(core_ref[0] * HALF, HALF), HALF)
        pairs = [(grads_hbm, grads_ref), (weights_hbm, weights_ref), (leaf_hbm, leaf_ref)]
        pairs += [(codes_hbm.at[rows, ours], whole_ref.at[rows, :]) for rows in row_cuts()]
        arriving = [pltpu.make_async_copy(a, b, sems.at[i]) for i, (a, b) in enumerate(pairs)]
        for copy in arriving:
            copy.start()
        for copy in arriving[:3]:
            copy.wait()
        weight, leaf = value_rows(weights_ref[...], leaf_ref[...])
        spread_values(grads_ref[...].astype(F32), weight, leaf, data_ref)
        codes_arriving = list(zip(row_cuts(), arriving[3:]))
        count = len(codes_arriving) // 2
        for part, half in enumerate(ROW_HALVES):
            for rows, copy in codes_arriving[part * count : (part + 1) * count]:
                copy.wait()
                codes_ref[rows, :] = whole_ref[rows, :].astype(F32).astype(BF16)
            for i in range(2 * UNROLL):
                sums = bin_sums(step + i, codes_ref, data_ref, half)
                sums_ref[i] = sums_ref[i] + sums if part else sums

    @pl.when(step > 0)
    def _():
        for i in range(2 * UNROLL):
            sums_ref[i] = bin_sums(step * (2 * UNROLL) + i, codes_ref, data_ref)


def interleave(even, odd):
    even, odd = (v.T.reshape(PEERS // 2, 8, COLS) for v in (even, odd))
    low = iota(even.shape, 1) < OWNED
    first = jnp.where(low, even, pltpu.roll(odd, OWNED, 1))
    second = jnp.where(low, pltpu.roll(even, OWNED, 1), odd)
    return (first, second)


def both_kernel(rows_ref, sums_ref, out_ref, data_ref, total_ref, largest_ref, even_ref, odd_ref):
    step = pl.program_id(0)

    @pl.when(step == 0)
    def _():
        parts = [
            rows_ref[ROW_DEV + i * AUX : ROW_DEV + (i + 1) * AUX, :]
            for i in range(ROW_DEV // AUX_CHUNK)
        ]
        aux = jnp.concatenate(parts, axis=1).astype(F32)
        spread_values(*split_aux(aux), data_ref)
        largest_ref[...] = jnp.zeros(largest_ref.shape, F32)

    codes_ref = rows_ref.at[:ROW_DEV, :]
    for i in range(DEEPER):
        pair = step * DEEPER + i
        even = bin_sums(2 * pair, codes_ref, data_ref) + sums_ref[2 * i]
        odd = bin_sums(2 * pair + 1, codes_ref, data_ref) + sums_ref[2 * i + 1]
        at = pl.multiple_of(pair * 8, 8)
        for side, values in enumerate(interleave(even[:COLS], odd[:COLS])):
            total_ref[:, side, pl.ds(at, 8), :] = values
            largest_ref[:, side] = jnp.maximum(largest_ref[:, side], jnp.abs(values))
        even_ref[pl.ds(at, 8), :] = even[COLS:]
        odd_ref[pl.ds(at, 8), :] = odd[COLS:]

    @pl.when(step == PAIRS // DEEPER - 1)
    def _():
        low = iota((PEERS // 2, 8, COLS), 1) < OWNED
        for side, weights in enumerate(interleave(even_ref[...], odd_ref[...])):
            most = jnp.abs(weights)
            for lanes in (8, 16, 32, 64):
                most = jnp.maximum(most, pltpu.roll(most, lanes, 2))
            exp_g, exp_w = (exponents(largest_ref[:, side]), exponents(most))
            scale_g, scale_w = (jnp.exp2(BITS - exp_g), jnp.exp2(BITS - exp_w))
            twice = jnp.concatenate([scale_g, scale_g], axis=1)
            for i in range(COLS // 16):
                rows = slice(i * 16, (i + 1) * 16)
                out_ref[:, side, rows, :] = whole(total_ref[:, side, rows, :] * twice)
            last = [weights * scale_w, jnp.where(low, exp_g, exp_w)]
            out_ref[:, side, COLS:, :] = whole(jnp.concatenate(last, axis=1))


def exponents(magnitudes):
    most = jnp.maximum(magnitudes, pltpu.roll(magnitudes, OWNED, 1))
    return jnp.ceil(jnp.log2(jnp.maximum(most, 1e-30)) + 0.001)


def whole(values):
    return jnp.round(values).astype(I32).astype(jnp.int16)


HIST_COST = pl.CostEstimate(
    flops=2 * ROW_DEV * HALF * BINS * 256, bytes_accessed=8 << 20, transcendentals=0
)


def own_sums(core, codes, grads, weights, leaf):
    ins = [codes, grads, weights, leaf]
    return pl.pallas_call(
        own_kernel,
        grid=(PAIRS // UNROLL,),
        in_specs=[pl.BlockSpec(memory_space=pltpu.SMEM)]
        + [pl.BlockSpec(memory_space=pl.ANY)] * len(ins),
        out_specs=pl.BlockSpec((2 * UNROLL, SENT, HALF), lambda i: (i, 0, 0)),
        out_shape=jax.ShapeDtypeStruct((BINS, SENT, HALF), F32),
        scratch_shapes=[pltpu.VMEM((ROW_DEV, HALF), I32)]
        + [pltpu.VMEM(a.shape, a.dtype) for a in ins[1:]]
        + [
            pltpu.VMEM((ROW_DEV, HALF), BF16),
            pltpu.VMEM((COLS + TARGETS, ROW_DEV), BF16),
            pltpu.SemaphoreType.DMA((ROW_DEV // ROW_BLOCK + 3,)),
        ],
        compiler_params=params(36),
        cost_estimate=HIST_COST,
    )(core, *[in_hbm(a) for a in ins])


def both_sums(rows, sums):
    halved = (PEERS // 2, 2)
    out = pl.pallas_call(
        both_kernel,
        grid=(PAIRS // DEEPER,),
        in_specs=[
            pl.BlockSpec(rows.shape, lambda i: (0, 0), pipeline_mode=pl.Buffered(1)),
            pl.BlockSpec((2 * DEEPER, SENT, HALF), lambda i: (i, 0, 0)),
        ],
        out_specs=pl.BlockSpec((*halved, MESSAGE, COLS), lambda i: (0, 0, 0, 0)),
        out_shape=pltpu.HBM((*halved, MESSAGE, COLS), jnp.int16),
        scratch_shapes=[
            pltpu.VMEM((COLS + TARGETS, ROW_DEV), BF16),
            pltpu.VMEM((*halved, COLS, COLS), F32),
            pltpu.VMEM((*halved, 8, COLS), F32),
            pltpu.VMEM((COLS, HALF), F32),
            pltpu.VMEM((COLS, HALF), F32),
        ],
        compiler_params=params(40),
        cost_estimate=HIST_COST,
    )(rows, sums)
    return out.reshape(PEERS, MESSAGE, COLS)


def place_kernel(feature_ref, core_ref, bin_ref, aux_ref, codes_ref, keep_ref, give_ref):
    core = core_ref[0]
    grads, weights, leaf = split_aux(aux_ref[...].astype(F32))
    chosen = jnp.where(iota((8, 128), 1) == (feature_ref[0] & 127), 1.0, 0.0).astype(BF16)
    column = lax.dot_general(
        chosen,
        codes_ref[...].astype(F32).astype(BF16),
        (((1,), (1,)), ((), ())),
        preferred_element_type=F32,
    )[0:1]
    child = jnp.where(column > bin_ref[0].astype(F32), 1.0, 0.0)
    key = leaf * 2 + child
    keys = 2 * LEAVES
    hot = jnp.where(iota((keys, ROW_DEV), 0).astype(F32) == key, 1.0, 0.0)
    width = 256
    earlier = jnp.where(iota((width, width), 0) < iota((width, width), 1), 1.0, 0.0).astype(BF16)
    counts = jnp.zeros((keys, 1), F32)
    ranks = []
    for i in range(ROW_DEV // width):
        part = hot[:, i * width : (i + 1) * width]
        before = jnp.dot(part.astype(BF16), earlier, preferred_element_type=F32) + counts
        ranks.append(jnp.sum(part * before, axis=0, keepdims=True))
        counts = counts + jnp.sum(part, axis=1, keepdims=True)
    rank = jnp.concatenate(ranks, axis=1)
    sibling = iota((keys, ROW_DEV), 0).astype(F32) == leaf * 2
    first = jnp.sum(jnp.where(sibling, counts, 0.0), axis=0, keepdims=True)
    slot = (leaf * CAP + rank + child * first).astype(I32)
    dims = (((1,), (1,)), ((), ()))
    group = 128 // TARGETS
    tiled = jnp.concatenate([grads] * group, axis=0)
    values = jnp.where(iota((128, 1), 0) >> 4 == (slot & (group - 1)), tiled, 0.0).astype(BF16)
    lines = CAP // group
    line = iota((lines, 1), 0)
    for l in range(LEAVES):
        target = 2 * (l % 4) + (core if l < 4 else 1 - core)
        out_ref = keep_ref if l < 4 else give_ref
        pick = jnp.where(line == (slot >> 3) - target * lines, 1.0, 0.0).astype(BF16)
        moved = lax.dot_general(pick, values, dims, preferred_element_type=F32)
        out_ref[l % 4, :COLS, :] = moved.astype(BF16)
    lane_values = jnp.where(iota((128, 1), 0) == (slot & 127), weights, 0.0).astype(BF16)
    blocks = CAP // 128
    for l in range(LEAVES):
        target = 2 * (l % 4) + (core if l < 4 else 1 - core)
        out_ref = keep_ref if l < 4 else give_ref
        pick = jnp.where(iota((16, 1), 0) == (slot >> 7) - target * blocks, 1.0, 0.0)
        pick = jnp.where(iota((16, 1), 0) < blocks, pick, 0.0).astype(BF16)
        moved = lax.dot_general(pick, lane_values, dims, preferred_element_type=F32)
        out_ref[l % 4, COLS:, :] = moved.astype(BF16)


def place_rows(split_feature, core, split_bin, aux, codes):
    smem = pl.BlockSpec(memory_space=pltpu.SMEM)
    block = jax.ShapeDtypeStruct((LEAVES // 2, COLS + 16, 128), BF16)
    spec = pl.BlockSpec(block.shape, lambda i, feature: (0, 0, 0))
    return pl.pallas_call(
        place_kernel,
        grid_spec=pltpu.PrefetchScalarGridSpec(
            num_scalar_prefetch=1,
            grid=(1,),
            in_specs=[
                smem,
                smem,
                pl.BlockSpec(aux.shape, lambda i, feature: (0, 0)),
                pl.BlockSpec((ROW_DEV, 128), lambda i, feature: (0, feature[0] >> 7)),
            ],
            out_specs=[spec, spec],
        ),
        out_shape=[block, block],
        compiler_params=params(56),
        cost_estimate=pl.CostEstimate(
            flops=2 * LEAVES * CAP * ROW_DEV * 32, bytes_accessed=1 << 20, transcendentals=0
        ),
    )(split_feature, core, split_bin, aux, codes)


def deliver(keep, give):
    core, chip = (lax.axis_index("grp_1"), lax.axis_index("grp_0"))
    got = lax.ppermute(give, "grp_1", [(0, 1), (1, 0)])
    first = jnp.where(core == 0, keep, got)
    second = jnp.where(core == 0, got, keep)
    blocks = jnp.stack([first, second], axis=1)
    arrived = []
    for s in range(4):
        block = lax.dynamic_index_in_dim(blocks, (chip + s) % 4, 0, keepdims=False)
        if s:
            block = lax.ppermute(block, "grp_0", [(i, (i + s) % 4) for i in range(4)])
        arrived.append(block)
    turned = jnp.stack([arrived[0], arrived[3], arrived[2], arrived[1]] * 2)
    ordered = lax.dynamic_slice_in_dim(turned, (4 - chip) % 4, 4, 0)
    return ordered.reshape(8, COLS + 16, 128)


def gain_kernel(parts_ref, out_ref):
    upper = iota((8, COLS), 0) < OWNED

    def add_part(p, so_far):
        tail = parts_ref[p, COLS:, :].astype(I32).astype(F32)
        powers = jnp.exp2(tail[8:] - BITS)
        turned = pltpu.roll(powers, OWNED, 0)
        scale_g = jnp.where(upper, powers, turned)
        scale_w = jnp.where(upper, turned, powers)
        values = parts_ref[p, :COLS, :].astype(I32).astype(F32)
        added = [so_far[i] + values[i * 8 : (i + 1) * 8] * scale_g for i in range(PAIRS)]
        return (*added, so_far[PAIRS] + tail[:8] * scale_w)

    start = tuple(jnp.zeros((8, COLS), F32) for _ in range(PAIRS + 1))
    total = lax.fori_loop(0, PEERS, add_part, start, unroll=4)
    expand = jnp.where(
        iota((COLS, 1), 0) == iota((1, PAIRS * COLS), 1) >> 4, 1.0, 0.0
    )
    spread_w = jnp.dot(
        total[PAIRS], expand, preferred_element_type=F32, precision=lax.Precision.HIGHEST
    )
    grads = total[:PAIRS]
    weights = [spread_w[:, i * COLS : (i + 1) * COLS] for i in range(PAIRS)]
    row = iota((8, COLS), 0)
    even = row < OWNED

    def sides(values):
        swapped = [pltpu.roll(v, OWNED, 0) for v in values]
        both = [v + s for v, s in zip(values, swapped)]
        left, right = ([], [])
        below = jnp.zeros((8, COLS), F32)
        for v, b in zip(values, both):
            left.append(below + jnp.where(even, v, b))
            below = below + b
        above = jnp.zeros((8, COLS), F32)
        for s, b in zip(reversed(swapped), reversed(both)):
            right.append(above + jnp.where(even, s, 0.0))
            above = above + b
        return (left, right[::-1])

    left_g, right_g = sides(grads)
    left_w, right_w = sides(weights)
    place = (row & (OWNED - 1)) * BINS + (row >> 2)
    gains = jnp.zeros((8, COLS), F32)
    for i in range(PAIRS):
        x, y = (left_w[i] + 1.0, right_w[i] + 1.0)
        diff = left_g[i] * y - right_g[i] * x
        terms = diff * diff / (x * y * (x + y))
        sums = jnp.sum(terms, axis=1, keepdims=True)
        gains = gains + jnp.where(iota((8, COLS), 1) == place + 2 * i, sums, 0.0)
    gains = jnp.sum(gains, axis=0, keepdims=True) / (LEAVES * TARGETS)
    out_ref[...] = jnp.broadcast_to(gains[None], out_ref.shape)


def owned_gains(parts):
    shape = (2 * PEERS, 1, OWNED * BINS)
    return pl.pallas_call(
        gain_kernel,
        out_shape=jax.ShapeDtypeStruct(shape, F32),
        in_specs=[pl.BlockSpec(parts.shape, lambda: (0, 0, 0))],
        out_specs=pl.BlockSpec(shape, lambda: (0, 0, 0)),
        compiler_params=params(16),
    )(parts)


def close_kernel(group_ref, gains_ref, table_ref, best_ref):
    group = group_ref[0]
    first = (group & 7) * 16 + (group >> 3)
    for i in range(8):
        table_ref[i] = gains_ref[first + 2 * i]
    highest = jnp.max(gains_ref[...], axis=0)
    best_ref[...] = jnp.max(highest, axis=1, keepdims=True)


def close(group, gains):
    return pl.pallas_call(
        close_kernel,
        out_shape=[
            jax.ShapeDtypeStruct((8, 1, OWNED * BINS), F32),
            jax.ShapeDtypeStruct((1, 1), F32),
        ],
        in_specs=[
            pl.BlockSpec(memory_space=pltpu.SMEM),
            pl.BlockSpec(gains.shape, lambda: (0, 0, 0)),
        ],
        out_specs=[
            pl.BlockSpec((8, 1, OWNED * BINS), lambda: (0, 0, 0)),
            pl.BlockSpec((1, 1), lambda: (0, 0)),
        ],
        compiler_params=params(4),
    )(group, gains)


def exchange(blocks, axis):
    return lax.all_to_all(blocks, axis, split_axis=0, concat_axis=0, tiled=True)


def shards(bin_codes, leaf_index, gradients, row_weights, split_feature, split_bin):
    core = lax.axis_index("grp_1").astype(I32).reshape(1)
    values = (gradients.T, row_weights.reshape(ROW_DEV // 128, 128), leaf_index.reshape(1, ROW_DEV))
    send, aux = prep(core, bin_codes, *values)
    other = lax.ppermute(send, "grp_1", [(0, 1), (1, 0)])
    sums = both_sums(other, own_sums(core, bin_codes, *values))
    arrived = exchange(sums, CHIPS)
    aux, unused = lax.optimization_barrier((aux, sums))
    moved = deliver(*place_rows(split_feature, core, split_bin, aux, bin_codes))
    everyone = exchange(owned_gains(arrived), ROWS_GRP)
    table, best = close(lax.axis_index(ROWS).astype(I32).reshape(1), everyone)
    table, best = (table.reshape(-1), best.reshape(1))
    moved_gradients = moved[:, :COLS].reshape(1, -1)
    moved_weights = moved[:, COLS : COLS + 8].reshape(1, -1)
    return (table, best, moved_gradients, moved_weights)


def solution(mesh):
    torus = Mesh(mesh.devices.reshape(4, 4, 4, 2), ("rows_0", "rows_1", "grp_0", "grp_1"))
    in_specs = (P(ROWS_GRP, None), P(ROWS_GRP, None), P(ROWS_GRP, None), P(ROWS_GRP), P(), P())
    out_specs = (P(ROWS), P(), P(ROWS_GRP, None), P(ROWS_GRP, None))
    return jax.shard_map(
        shards, mesh=torus, in_specs=in_specs, out_specs=out_specs, check_vma=False
    )
```

```python
import jax
import jax.numpy as jnp
from jax import lax
from jax.experimental import pallas as pl
from jax.experimental.pallas import tpu as pltpu
from jax.sharding import Mesh
from jax.sharding import PartitionSpec as P

BINS = 32
TARGETS = 16
LEAVES = 8
CAP = 1024
COLS = LEAVES * TARGETS
FEATURES = 512
HALF = FEATURES // 2
ROW_DEV = 4096
ROW_BLOCK = 512
PEERS = 64
OWNED = 4
PAIRS = BINS // 2
AUX = 32
AUX_CHUNK = HALF
AUX_ROWS = ROW_DEV // AUX_CHUNK * AUX
SENT = COLS + LEAVES
GRP = ("grp_0", "grp_1")
ROWS_GRP = ("rows_0", "rows_1", "grp_0", "grp_1")
ROWS = ("rows_0", "rows_1")
CHIPS = ("rows_0", "rows_1", "grp_0")
F32 = jnp.float32
BF16 = jnp.bfloat16
I32 = jnp.int32


def iota(shape, dim):
    return lax.broadcasted_iota(I32, shape, dim)


def in_hbm(array):
    return pltpu.with_memory_space_constraint(array, pltpu.HBM)


def params(mib):
    return pltpu.CompilerParams(vmem_limit_bytes=mib << 20)


def value_rows(weights, leaf):
    lines = weights.astype(F32)
    weight = jnp.concatenate([lines[i : i + 1] for i in range(lines.shape[0])], axis=1)
    return (weight, leaf.astype(F32))


def prep_kernel(
    core_ref, codes_hbm, grads_hbm, weights_hbm, leaf_hbm, send_hbm, aux_hbm,
    codes_ref, grads_ref, weights_ref, leaf_ref, send_ref, aux_ref, in_sems, out_sems,
):
    cuts = row_cuts()
    theirs = pl.ds(pl.multiple_of((1 - core_ref[0]) * HALF, HALF), HALF)
    pairs = [(grads_hbm, grads_ref), (weights_hbm, weights_ref), (leaf_hbm, leaf_ref)]
    pairs += [(codes_hbm.at[rows, theirs], codes_ref.at[rows, :]) for rows in cuts]
    arriving = [pltpu.make_async_copy(a, b, in_sems.at[i]) for i, (a, b) in enumerate(pairs)]
    for copy in arriving:
        copy.start()
    leaving = []

    def leave(source, target):
        copy = pltpu.make_async_copy(source, target, out_sems.at[len(leaving)])
        copy.start()
        leaving.append(copy)

    for copy in arriving[:3]:
        copy.wait()
    weight, leaf = value_rows(weights_ref[...], leaf_ref[...])
    row = iota((TARGETS, ROW_DEV), 0)
    rest = jnp.where(row == 0, weight, jnp.where(row == 1, leaf, 0.0)).astype(BF16)
    aux_ref[:TARGETS, :] = grads_ref[...]
    aux_ref[TARGETS:, :] = rest
    leave(aux_ref, aux_hbm)
    for i in range(ROW_DEV // AUX_CHUNK):
        lanes = slice(i * AUX_CHUNK, (i + 1) * AUX_CHUNK)
        at = ROW_DEV + i * AUX
        send_ref[at : at + TARGETS, :] = grads_ref[:, lanes]
        send_ref[at + TARGETS : at + AUX, :] = rest[:, lanes]
    leave(send_ref.at[ROW_DEV:, :], send_hbm.at[ROW_DEV:, :])
    for rows, copy in zip(cuts, arriving[3:]):
        copy.wait()
        send_ref[rows, :] = codes_ref[rows, :].astype(F32).astype(BF16)
        leave(send_ref.at[rows, :], send_hbm.at[rows, :])
    for copy in leaving:
        copy.wait()


def row_cuts():
    return [slice(i * ROW_BLOCK, (i + 1) * ROW_BLOCK) for i in range(ROW_DEV // ROW_BLOCK)]


def spread_values(grads, weights, leaf, data_ref):
    for l in range(LEAVES):
        data_ref[l * TARGETS : (l + 1) * TARGETS, :] = jnp.where(leaf == l, grads, 0.0).astype(BF16)
    ids = iota((TARGETS, ROW_DEV), 0).astype(F32)
    data_ref[COLS : COLS + TARGETS, :] = jnp.where(leaf == ids, weights, 0.0).astype(BF16)


def prep(core, codes, grads, weights, leaf):
    blocks = ROW_DEV // ROW_BLOCK
    there = pl.BlockSpec(memory_space=pl.ANY)
    outs = [(ROW_DEV + AUX_ROWS, HALF), (AUX, ROW_DEV)]
    ins = [codes, grads, weights, leaf]
    return pl.pallas_call(
        prep_kernel,
        in_specs=[pl.BlockSpec(memory_space=pltpu.SMEM)] + [there] * len(ins),
        out_specs=[there] * len(outs),
        out_shape=[pltpu.HBM(shape, BF16) for shape in outs],
        scratch_shapes=[pltpu.VMEM((ROW_DEV, HALF), I32)]
        + [pltpu.VMEM(a.shape, a.dtype) for a in ins[1:]]
        + [pltpu.VMEM(shape, BF16) for shape in outs]
        + [pltpu.SemaphoreType.DMA((blocks + 3,)), pltpu.SemaphoreType.DMA((blocks + 2,))],
        compiler_params=params(32),
        cost_estimate=pl.CostEstimate(
            flops=ROW_DEV * HALF, bytes_accessed=ROW_DEV * HALF * 6, transcendentals=0
        ),
    )(core, *[in_hbm(a) for a in ins])


def split_aux(aux):
    return (aux[:TARGETS], aux[TARGETS : TARGETS + 1], aux[TARGETS + 1 : TARGETS + 2])


def bin_sums(index, codes_ref, data_ref, rows=slice(None)):
    wanted = jnp.full((1, HALF), 0.0, F32) + index.astype(F32)
    codes = codes_ref[rows, :]
    hot = jnp.where(codes == wanted.astype(BF16), jnp.ones((), BF16), jnp.zeros((), BF16))
    return jnp.dot(data_ref[:, rows], hot, preferred_element_type=F32)[:SENT]


ROW_HALVES = (slice(0, ROW_DEV // 2), slice(ROW_DEV // 2, ROW_DEV))


UNROLL = 4
DEEPER = 8
BITS = 15.0
MESSAGE = COLS + 16


def own_kernel(
    core_ref, codes_hbm, grads_hbm, weights_hbm, leaf_hbm, sums_ref,
    whole_ref, grads_ref, weights_ref, leaf_ref, codes_ref, data_ref, sems,
):
    step = pl.program_id(0)

    @pl.when(step == 0)
    def _():
        ours = pl.ds(pl.multiple_of(core_ref[0] * HALF, HALF), HALF)
        pairs = [(grads_hbm, grads_ref), (weights_hbm, weights_ref), (leaf_hbm, leaf_ref)]
        pairs += [(codes_hbm.at[rows, ours], whole_ref.at[rows, :]) for rows in row_cuts()]
        arriving = [pltpu.make_async_copy(a, b, sems.at[i]) for i, (a, b) in enumerate(pairs)]
        for copy in arriving:
            copy.start()
        for copy in arriving[:3]:
            copy.wait()
        weight, leaf = value_rows(weights_ref[...], leaf_ref[...])
        spread_values(grads_ref[...].astype(F32), weight, leaf, data_ref)
        codes_arriving = list(zip(row_cuts(), arriving[3:]))
        count = len(codes_arriving) // 2
        for part, half in enumerate(ROW_HALVES):
            for rows, copy in codes_arriving[part * count : (part + 1) * count]:
                copy.wait()
                codes_ref[rows, :] = whole_ref[rows, :].astype(F32).astype(BF16)
            for i in range(2 * UNROLL):
                sums = bin_sums(step + i, codes_ref, data_ref, half)
                sums_ref[i] = sums_ref[i] + sums if part else sums

    @pl.when(step > 0)
    def _():
        for i in range(2 * UNROLL):
            sums_ref[i] = bin_sums(step * (2 * UNROLL) + i, codes_ref, data_ref)


def interleave(even, odd):
    even, odd = (v.T.reshape(PEERS // 2, 8, COLS) for v in (even, odd))
    low = iota(even.shape, 1) < OWNED
    first = jnp.where(low, even, pltpu.roll(odd, OWNED, 1))
    second = jnp.where(low, pltpu.roll(even, OWNED, 1), odd)
    return (first, second)


def both_kernel(rows_ref, sums_ref, out_ref, data_ref, total_ref, largest_ref, even_ref, odd_ref):
    step = pl.program_id(0)

    @pl.when(step == 0)
    def _():
        parts = [
            rows_ref[ROW_DEV + i * AUX : ROW_DEV + (i + 1) * AUX, :]
            for i in range(ROW_DEV // AUX_CHUNK)
        ]
        aux = jnp.concatenate(parts, axis=1).astype(F32)
        spread_values(*split_aux(aux), data_ref)
        largest_ref[...] = jnp.zeros(largest_ref.shape, F32)

    codes_ref = rows_ref.at[:ROW_DEV, :]
    for i in range(DEEPER):
        pair = step * DEEPER + i
        even = bin_sums(2 * pair, codes_ref, data_ref) + sums_ref[2 * i]
        odd = bin_sums(2 * pair + 1, codes_ref, data_ref) + sums_ref[2 * i + 1]
        at = pl.multiple_of(pair * 8, 8)
        for side, values in enumerate(interleave(even[:COLS], odd[:COLS])):
            total_ref[:, side, pl.ds(at, 8), :] = values
            largest_ref[:, side] = jnp.maximum(largest_ref[:, side], jnp.abs(values))
        even_ref[pl.ds(at, 8), :] = even[COLS:]
        odd_ref[pl.ds(at, 8), :] = odd[COLS:]

    @pl.when(step == PAIRS // DEEPER - 1)
    def _():
        low = iota((PEERS // 2, 8, COLS), 1) < OWNED
        for side, weights in enumerate(interleave(even_ref[...], odd_ref[...])):
            most = jnp.abs(weights)
            for lanes in (8, 16, 32, 64):
                most = jnp.maximum(most, pltpu.roll(most, lanes, 2))
            exp_g, exp_w = (exponents(largest_ref[:, side]), exponents(most))
            scale_g, scale_w = (jnp.exp2(BITS - exp_g), jnp.exp2(BITS - exp_w))
            twice = jnp.concatenate([scale_g, scale_g], axis=1)
            for i in range(COLS // 16):
                rows = slice(i * 16, (i + 1) * 16)
                out_ref[:, side, rows, :] = whole(total_ref[:, side, rows, :] * twice)
            last = [weights * scale_w, jnp.where(low, exp_g, exp_w)]
            out_ref[:, side, COLS:, :] = whole(jnp.concatenate(last, axis=1))


def exponents(magnitudes):
    most = jnp.maximum(magnitudes, pltpu.roll(magnitudes, OWNED, 1))
    return jnp.ceil(jnp.log2(jnp.maximum(most, 1e-30)) + 0.001)


def whole(values):
    return jnp.round(values).astype(I32).astype(jnp.int16)


HIST_COST = pl.CostEstimate(
    flops=2 * ROW_DEV * HALF * BINS * 256, bytes_accessed=8 << 20, transcendentals=0
)


def own_sums(core, codes, grads, weights, leaf):
    ins = [codes, grads, weights, leaf]
    return pl.pallas_call(
        own_kernel,
        grid=(PAIRS // UNROLL,),
        in_specs=[pl.BlockSpec(memory_space=pltpu.SMEM)]
        + [pl.BlockSpec(memory_space=pl.ANY)] * len(ins),
        out_specs=pl.BlockSpec((2 * UNROLL, SENT, HALF), lambda i: (i, 0, 0)),
        out_shape=jax.ShapeDtypeStruct((BINS, SENT, HALF), F32),
        scratch_shapes=[pltpu.VMEM((ROW_DEV, HALF), I32)]
        + [pltpu.VMEM(a.shape, a.dtype) for a in ins[1:]]
        + [
            pltpu.VMEM((ROW_DEV, HALF), BF16),
            pltpu.VMEM((COLS + TARGETS, ROW_DEV), BF16),
            pltpu.SemaphoreType.DMA((ROW_DEV // ROW_BLOCK + 3,)),
        ],
        compiler_params=params(36),
        cost_estimate=HIST_COST,
    )(core, *[in_hbm(a) for a in ins])


def both_sums(rows, sums):
    halved = (PEERS // 2, 2)
    out = pl.pallas_call(
        both_kernel,
        grid=(PAIRS // DEEPER,),
        in_specs=[
            pl.BlockSpec(rows.shape, lambda i: (0, 0), pipeline_mode=pl.Buffered(1)),
            pl.BlockSpec((2 * DEEPER, SENT, HALF), lambda i: (i, 0, 0)),
        ],
        out_specs=pl.BlockSpec((*halved, MESSAGE, COLS), lambda i: (0, 0, 0, 0)),
        out_shape=pltpu.HBM((*halved, MESSAGE, COLS), jnp.int16),
        scratch_shapes=[
            pltpu.VMEM((COLS + TARGETS, ROW_DEV), BF16),
            pltpu.VMEM((*halved, COLS, COLS), F32),
            pltpu.VMEM((*halved, 8, COLS), F32),
            pltpu.VMEM((COLS, HALF), F32),
            pltpu.VMEM((COLS, HALF), F32),
        ],
        compiler_params=params(40),
        cost_estimate=HIST_COST,
    )(rows, sums)
    return out.reshape(PEERS, MESSAGE, COLS)


def place_kernel(feature_ref, core_ref, bin_ref, aux_ref, codes_ref, keep_ref, give_ref):
    core = core_ref[0]
    grads, weights, leaf = split_aux(aux_ref[...].astype(F32))
    chosen = jnp.where(iota((8, 128), 1) == (feature_ref[0] & 127), 1.0, 0.0).astype(BF16)
    column = lax.dot_general(
        chosen,
        codes_ref[...].astype(F32).astype(BF16),
        (((1,), (1,)), ((), ())),
        preferred_element_type=F32,
    )[0:1]
    child = jnp.where(column > bin_ref[0].astype(F32), 1.0, 0.0)
    key = leaf * 2 + child
    keys = 2 * LEAVES
    hot = jnp.where(iota((keys, ROW_DEV), 0).astype(F32) == key, 1.0, 0.0)
    width = 256
    earlier = jnp.where(iota((width, width), 0) < iota((width, width), 1), 1.0, 0.0).astype(BF16)
    counts = jnp.zeros((keys, 1), F32)
    ranks = []
    for i in range(ROW_DEV // width):
        part = hot[:, i * width : (i + 1) * width]
        before = jnp.dot(part.astype(BF16), earlier, preferred_element_type=F32) + counts
        ranks.append(jnp.sum(part * before, axis=0, keepdims=True))
        counts = counts + jnp.sum(part, axis=1, keepdims=True)
    rank = jnp.concatenate(ranks, axis=1)
    sibling = iota((keys, ROW_DEV), 0).astype(F32) == leaf * 2
    first = jnp.sum(jnp.where(sibling, counts, 0.0), axis=0, keepdims=True)
    slot = (leaf * CAP + rank + child * first).astype(I32)
    dims = (((1,), (1,)), ((), ()))
    group = 128 // TARGETS
    tiled = jnp.concatenate([grads] * group, axis=0)
    values = jnp.where(iota((128, 1), 0) >> 4 == (slot & (group - 1)), tiled, 0.0).astype(BF16)
    lines = CAP // group
    line = iota((lines, 1), 0)
    for l in range(LEAVES):
        target = 2 * (l % 4) + (core if l < 4 else 1 - core)
        out_ref = keep_ref if l < 4 else give_ref
        pick = jnp.where(line == (slot >> 3) - target * lines, 1.0, 0.0).astype(BF16)
        moved = lax.dot_general(pick, values, dims, preferred_element_type=F32)
        out_ref[l % 4, :COLS, :] = moved.astype(BF16)
    lane_values = jnp.where(iota((128, 1), 0) == (slot & 127), weights, 0.0).astype(BF16)
    blocks = CAP // 128
    for l in range(LEAVES):
        target = 2 * (l % 4) + (core if l < 4 else 1 - core)
        out_ref = keep_ref if l < 4 else give_ref
        pick = jnp.where(iota((16, 1), 0) == (slot >> 7) - target * blocks, 1.0, 0.0)
        pick = jnp.where(iota((16, 1), 0) < blocks, pick, 0.0).astype(BF16)
        moved = lax.dot_general(pick, lane_values, dims, preferred_element_type=F32)
        out_ref[l % 4, COLS:, :] = moved.astype(BF16)


def place_rows(split_feature, core, split_bin, aux, codes):
    smem = pl.BlockSpec(memory_space=pltpu.SMEM)
    block = jax.ShapeDtypeStruct((LEAVES // 2, COLS + 16, 128), BF16)
    spec = pl.BlockSpec(block.shape, lambda i, feature: (0, 0, 0))
    return pl.pallas_call(
        place_kernel,
        grid_spec=pltpu.PrefetchScalarGridSpec(
            num_scalar_prefetch=1,
            grid=(1,),
            in_specs=[
                smem,
                smem,
                pl.BlockSpec(aux.shape, lambda i, feature: (0, 0)),
                pl.BlockSpec((ROW_DEV, 128), lambda i, feature: (0, feature[0] >> 7)),
            ],
            out_specs=[spec, spec],
        ),
        out_shape=[block, block],
        compiler_params=params(56),
        cost_estimate=pl.CostEstimate(
            flops=2 * LEAVES * CAP * ROW_DEV * 32, bytes_accessed=1 << 20, transcendentals=0
        ),
    )(split_feature, core, split_bin, aux, codes)


def deliver(keep, give, gains):
    core, chip = (lax.axis_index("grp_1"), lax.axis_index("grp_0"))
    got = lax.ppermute(give, "grp_1", [(0, 1), (1, 0)])
    first = jnp.where(core == 0, keep, got)
    second = jnp.where(core == 0, got, keep)
    blocks = jnp.stack([first, second], axis=1)
    arrived = []
    for s in range(4):
        block = lax.dynamic_index_in_dim(blocks, (chip + s) % 4, 0, keepdims=False)
        if s:
            block = lax.ppermute(block, "grp_0", [(i, (i + s) % 4) for i in range(4)])
        arrived.append(block)
    *arrived, gains = lax.optimization_barrier((*arrived, gains))
    turned = jnp.stack([arrived[0], arrived[3], arrived[2], arrived[1]] * 2)
    ordered = lax.dynamic_slice_in_dim(turned, (4 - chip) % 4, 4, 0)
    return ordered.reshape(8, COLS + 16, 128)


def gain_kernel(parts_ref, out_ref):
    upper = iota((8, COLS), 0) < OWNED

    def add_part(p, so_far):
        tail = parts_ref[p, COLS:, :].astype(I32).astype(F32)
        powers = jnp.exp2(tail[8:] - BITS)
        turned = pltpu.roll(powers, OWNED, 0)
        scale_g = jnp.where(upper, powers, turned)
        scale_w = jnp.where(upper, turned, powers)
        values = parts_ref[p, :COLS, :].astype(I32).astype(F32)
        added = [so_far[i] + values[i * 8 : (i + 1) * 8] * scale_g for i in range(PAIRS)]
        return (*added, so_far[PAIRS] + tail[:8] * scale_w)

    start = tuple(jnp.zeros((8, COLS), F32) for _ in range(PAIRS + 1))
    total = lax.fori_loop(0, PEERS, add_part, start, unroll=4)
    expand = jnp.where(
        iota((COLS, 1), 0) == iota((1, PAIRS * COLS), 1) >> 4, 1.0, 0.0
    )
    spread_w = jnp.dot(
        total[PAIRS], expand, preferred_element_type=F32, precision=lax.Precision.HIGHEST
    )
    grads = total[:PAIRS]
    weights = [spread_w[:, i * COLS : (i + 1) * COLS] for i in range(PAIRS)]
    row = iota((8, COLS), 0)
    even = row < OWNED

    def sides(values):
        swapped = [pltpu.roll(v, OWNED, 0) for v in values]
        both = [v + s for v, s in zip(values, swapped)]
        left, right = ([], [])
        below = jnp.zeros((8, COLS), F32)
        for v, b in zip(values, both):
            left.append(below + jnp.where(even, v, b))
            below = below + b
        above = jnp.zeros((8, COLS), F32)
        for s, b in zip(reversed(swapped), reversed(both)):
            right.append(above + jnp.where(even, s, 0.0))
            above = above + b
        return (left, right[::-1])

    left_g, right_g = sides(grads)
    left_w, right_w = sides(weights)
    place = (row & (OWNED - 1)) * BINS + (row >> 2)
    gains = jnp.zeros((8, COLS), F32)
    for i in range(PAIRS):
        x, y = (left_w[i] + 1.0, right_w[i] + 1.0)
        diff = left_g[i] * y - right_g[i] * x
        terms = diff * diff / (x * y * (x + y))
        sums = jnp.sum(terms, axis=1, keepdims=True)
        gains = gains + jnp.where(iota((8, COLS), 1) == place + 2 * i, sums, 0.0)
    gains = jnp.sum(gains, axis=0, keepdims=True) / (LEAVES * TARGETS)
    out_ref[...] = jnp.broadcast_to(gains[None], out_ref.shape)


def owned_gains(parts):
    shape = (2 * PEERS, 1, OWNED * BINS)
    return pl.pallas_call(
        gain_kernel,
        out_shape=jax.ShapeDtypeStruct(shape, F32),
        in_specs=[pl.BlockSpec(parts.shape, lambda: (0, 0, 0))],
        out_specs=pl.BlockSpec(shape, lambda: (0, 0, 0)),
        compiler_params=params(16),
    )(parts)


def close_kernel(group_ref, gains_ref, table_ref, best_ref):
    group = group_ref[0]
    first = (group & 7) * 16 + (group >> 3)
    for i in range(8):
        table_ref[i] = gains_ref[first + 2 * i]
    highest = jnp.max(gains_ref[...], axis=0)
    best_ref[...] = jnp.max(highest, axis=1, keepdims=True)


def close(group, gains):
    return pl.pallas_call(
        close_kernel,
        out_shape=[
            jax.ShapeDtypeStruct((8, 1, OWNED * BINS), F32),
            jax.ShapeDtypeStruct((1, 1), F32),
        ],
        in_specs=[
            pl.BlockSpec(memory_space=pltpu.SMEM),
            pl.BlockSpec(gains.shape, lambda: (0, 0, 0)),
        ],
        out_specs=[
            pl.BlockSpec((8, 1, OWNED * BINS), lambda: (0, 0, 0)),
            pl.BlockSpec((1, 1), lambda: (0, 0)),
        ],
        compiler_params=params(4),
    )(group, gains)


def exchange(blocks, axis):
    return lax.all_to_all(blocks, axis, split_axis=0, concat_axis=0, tiled=True)


def shards(bin_codes, leaf_index, gradients, row_weights, split_feature, split_bin):
    core = lax.axis_index("grp_1").astype(I32).reshape(1)
    values = (gradients.T, row_weights.reshape(ROW_DEV // 128, 128), leaf_index.reshape(1, ROW_DEV))
    send, aux = prep(core, bin_codes, *values)
    other = lax.ppermute(send, "grp_1", [(0, 1), (1, 0)])
    sums = both_sums(other, own_sums(core, bin_codes, *values))
    arrived = exchange(sums, CHIPS)
    aux, unused = lax.optimization_barrier((aux, sums))
    gains = owned_gains(arrived)
    moved = deliver(*place_rows(split_feature, core, split_bin, aux, bin_codes), gains)
    everyone = exchange(gains, ROWS_GRP)
    table, best = close(lax.axis_index(ROWS).astype(I32).reshape(1), everyone)
    table, best = (table.reshape(-1), best.reshape(1))
    moved_gradients = moved[:, :COLS].reshape(1, -1)
    moved_weights = moved[:, COLS : COLS + 8].reshape(1, -1)
    return (table, best, moved_gradients, moved_weights)


def solution(mesh):
    torus = Mesh(mesh.devices.reshape(4, 4, 4, 2), ("rows_0", "rows_1", "grp_0", "grp_1"))
    in_specs = (P(ROWS_GRP, None), P(ROWS_GRP, None), P(ROWS_GRP, None), P(ROWS_GRP), P(), P())
    out_specs = (P(ROWS), P(), P(ROWS_GRP, None), P(ROWS_GRP, None))
    return jax.shard_map(
        shards, mesh=torus, in_specs=in_specs, out_specs=out_specs, check_vma=False
    )
```

```python
import jax
import jax.numpy as jnp
from jax import lax
from jax.experimental import pallas as pl
from jax.experimental.pallas import tpu as pltpu
from jax.sharding import Mesh
from jax.sharding import PartitionSpec as P

BINS = 32
TARGETS = 16
LEAVES = 8
CAP = 1024
COLS = LEAVES * TARGETS
FEATURES = 512
HALF = FEATURES // 2
ROW_DEV = 4096
ROW_BLOCK = 512
PEERS = 64
OWNED = 4
PAIRS = BINS // 2
AUX = 32
AUX_CHUNK = HALF
AUX_ROWS = ROW_DEV // AUX_CHUNK * AUX
SENT = COLS + LEAVES
GRP = ("grp_0", "grp_1")
ROWS_GRP = ("rows_0", "rows_1", "grp_0", "grp_1")
ROWS = ("rows_0", "rows_1")
CHIPS = ("grp_0", "rows_0", "rows_1")
F32 = jnp.float32
BF16 = jnp.bfloat16
I32 = jnp.int32


def iota(shape, dim):
    return lax.broadcasted_iota(I32, shape, dim)


def in_hbm(array):
    return pltpu.with_memory_space_constraint(array, pltpu.HBM)


def params(mib):
    return pltpu.CompilerParams(vmem_limit_bytes=mib << 20)


def value_rows(weights, leaf):
    lines = weights.astype(F32)
    weight = jnp.concatenate([lines[i : i + 1] for i in range(lines.shape[0])], axis=1)
    return (weight, leaf.astype(F32))


def prep_kernel(
    core_ref, codes_hbm, grads_hbm, weights_hbm, leaf_hbm, send_hbm, aux_hbm,
    codes_ref, grads_ref, weights_ref, leaf_ref, send_ref, aux_ref, in_sems, out_sems,
):
    cuts = row_cuts()
    theirs = pl.ds(pl.multiple_of((1 - core_ref[0]) * HALF, HALF), HALF)
    pairs = [(grads_hbm, grads_ref), (weights_hbm, weights_ref), (leaf_hbm, leaf_ref)]
    pairs += [(codes_hbm.at[rows, theirs], codes_ref.at[rows, :]) for rows in cuts]
    arriving = [pltpu.make_async_copy(a, b, in_sems.at[i]) for i, (a, b) in enumerate(pairs)]
    for copy in arriving:
        copy.start()
    leaving = []

    def leave(source, target):
        copy = pltpu.make_async_copy(source, target, out_sems.at[len(leaving)])
        copy.start()
        leaving.append(copy)

    for copy in arriving[:3]:
        copy.wait()
    weight, leaf = value_rows(weights_ref[...], leaf_ref[...])
    row = iota((TARGETS, ROW_DEV), 0)
    rest = jnp.where(row == 0, weight, jnp.where(row == 1, leaf, 0.0)).astype(BF16)
    aux_ref[:TARGETS, :] = grads_ref[...]
    aux_ref[TARGETS:, :] = rest
    leave(aux_ref, aux_hbm)
    for i in range(ROW_DEV // AUX_CHUNK):
        lanes = slice(i * AUX_CHUNK, (i + 1) * AUX_CHUNK)
        at = ROW_DEV + i * AUX
        send_ref[at : at + TARGETS, :] = grads_ref[:, lanes]
        send_ref[at + TARGETS : at + AUX, :] = rest[:, lanes]
    leave(send_ref.at[ROW_DEV:, :], send_hbm.at[ROW_DEV:, :])
    for rows, copy in zip(cuts, arriving[3:]):
        copy.wait()
        send_ref[rows, :] = codes_ref[rows, :].astype(F32).astype(BF16)
        leave(send_ref.at[rows, :], send_hbm.at[rows, :])
    for copy in leaving:
        copy.wait()


def row_cuts():
    return [slice(i * ROW_BLOCK, (i + 1) * ROW_BLOCK) for i in range(ROW_DEV // ROW_BLOCK)]


def spread_values(grads, weights, leaf, data_ref):
    for l in range(LEAVES):
        data_ref[l * TARGETS : (l + 1) * TARGETS, :] = jnp.where(leaf == l, grads, 0.0).astype(BF16)
    ids = iota((TARGETS, ROW_DEV), 0).astype(F32)
    data_ref[COLS : COLS + TARGETS, :] = jnp.where(leaf == ids, weights, 0.0).astype(BF16)


def prep(core, codes, grads, weights, leaf):
    blocks = ROW_DEV // ROW_BLOCK
    there = pl.BlockSpec(memory_space=pl.ANY)
    outs = [(ROW_DEV + AUX_ROWS, HALF), (AUX, ROW_DEV)]
    ins = [codes, grads, weights, leaf]
    return pl.pallas_call(
        prep_kernel,
        in_specs=[pl.BlockSpec(memory_space=pltpu.SMEM)] + [there] * len(ins),
        out_specs=[there] * len(outs),
        out_shape=[pltpu.HBM(shape, BF16) for shape in outs],
        scratch_shapes=[pltpu.VMEM((ROW_DEV, HALF), I32)]
        + [pltpu.VMEM(a.shape, a.dtype) for a in ins[1:]]
        + [pltpu.VMEM(shape, BF16) for shape in outs]
        + [pltpu.SemaphoreType.DMA((blocks + 3,)), pltpu.SemaphoreType.DMA((blocks + 2,))],
        compiler_params=params(32),
        cost_estimate=pl.CostEstimate(
            flops=ROW_DEV * HALF, bytes_accessed=ROW_DEV * HALF * 6, transcendentals=0
        ),
    )(core, *[in_hbm(a) for a in ins])


def split_aux(aux):
    return (aux[:TARGETS], aux[TARGETS : TARGETS + 1], aux[TARGETS + 1 : TARGETS + 2])


def bin_sums(index, codes_ref, data_ref, rows=slice(None)):
    wanted = jnp.full((1, HALF), 0.0, F32) + index.astype(F32)
    codes = codes_ref[rows, :]
    hot = jnp.where(codes == wanted.astype(BF16), jnp.ones((), BF16), jnp.zeros((), BF16))
    return jnp.dot(data_ref[:, rows], hot, preferred_element_type=F32)[:SENT]


ROW_HALVES = (slice(0, ROW_DEV // 2), slice(ROW_DEV // 2, ROW_DEV))


UNROLL = 4
DEEPER = 8
BITS = 15.0
MESSAGE = COLS + 16


def own_kernel(
    core_ref, codes_hbm, grads_hbm, weights_hbm, leaf_hbm, sums_ref,
    whole_ref, grads_ref, weights_ref, leaf_ref, codes_ref, data_ref, sems,
):
    step = pl.program_id(0)

    @pl.when(step == 0)
    def _():
        ours = pl.ds(pl.multiple_of(core_ref[0] * HALF, HALF), HALF)
        pairs = [(grads_hbm, grads_ref), (weights_hbm, weights_ref), (leaf_hbm, leaf_ref)]
        pairs += [(codes_hbm.at[rows, ours], whole_ref.at[rows, :]) for rows in row_cuts()]
        arriving = [pltpu.make_async_copy(a, b, sems.at[i]) for i, (a, b) in enumerate(pairs)]
        for copy in arriving:
            copy.start()
        for copy in arriving[:3]:
            copy.wait()
        weight, leaf = value_rows(weights_ref[...], leaf_ref[...])
        spread_values(grads_ref[...].astype(F32), weight, leaf, data_ref)
        codes_arriving = list(zip(row_cuts(), arriving[3:]))
        count = len(codes_arriving) // 2
        for part, half in enumerate(ROW_HALVES):
            for rows, copy in codes_arriving[part * count : (part + 1) * count]:
                copy.wait()
                codes_ref[rows, :] = whole_ref[rows, :].astype(F32).astype(BF16)
            for i in range(2 * UNROLL):
                sums = bin_sums(step + i, codes_ref, data_ref, half)
                sums_ref[i] = sums_ref[i] + sums if part else sums

    @pl.when(step > 0)
    def _():
        for i in range(2 * UNROLL):
            sums_ref[i] = bin_sums(step * (2 * UNROLL) + i, codes_ref, data_ref)


def interleave(even, odd):
    even, odd = (v.T.reshape(PEERS // 2, 8, COLS) for v in (even, odd))
    low = iota(even.shape, 1) < OWNED
    first = jnp.where(low, even, pltpu.roll(odd, OWNED, 1))
    second = jnp.where(low, pltpu.roll(even, OWNED, 1), odd)
    return (first, second)


def both_kernel(rows_ref, sums_ref, out_ref, data_ref, total_ref, largest_ref, even_ref, odd_ref):
    step = pl.program_id(0)

    @pl.when(step == 0)
    def _():
        parts = [
            rows_ref[ROW_DEV + i * AUX : ROW_DEV + (i + 1) * AUX, :]
            for i in range(ROW_DEV // AUX_CHUNK)
        ]
        aux = jnp.concatenate(parts, axis=1).astype(F32)
        spread_values(*split_aux(aux), data_ref)
        largest_ref[...] = jnp.zeros(largest_ref.shape, F32)

    codes_ref = rows_ref.at[:ROW_DEV, :]
    for i in range(DEEPER):
        pair = step * DEEPER + i
        even = bin_sums(2 * pair, codes_ref, data_ref) + sums_ref[2 * i]
        odd = bin_sums(2 * pair + 1, codes_ref, data_ref) + sums_ref[2 * i + 1]
        at = pl.multiple_of(pair * 8, 8)
        for side, values in enumerate(interleave(even[:COLS], odd[:COLS])):
            total_ref[:, side, pl.ds(at, 8), :] = values
            largest_ref[:, side] = jnp.maximum(largest_ref[:, side], jnp.abs(values))
        even_ref[pl.ds(at, 8), :] = even[COLS:]
        odd_ref[pl.ds(at, 8), :] = odd[COLS:]

    @pl.when(step == PAIRS // DEEPER - 1)
    def _():
        low = iota((PEERS // 2, 8, COLS), 1) < OWNED
        for side, weights in enumerate(interleave(even_ref[...], odd_ref[...])):
            most = jnp.abs(weights)
            for lanes in (8, 16, 32, 64):
                most = jnp.maximum(most, pltpu.roll(most, lanes, 2))
            exp_g, exp_w = (exponents(largest_ref[:, side]), exponents(most))
            scale_g, scale_w = (jnp.exp2(BITS - exp_g), jnp.exp2(BITS - exp_w))
            twice = jnp.concatenate([scale_g, scale_g], axis=1)
            for i in range(COLS // 16):
                rows = slice(i * 16, (i + 1) * 16)
                out_ref[:, side, rows, :] = whole(total_ref[:, side, rows, :] * twice)
            last = [weights * scale_w, jnp.where(low, exp_g, exp_w)]
            out_ref[:, side, COLS:, :] = whole(jnp.concatenate(last, axis=1))


def exponents(magnitudes):
    most = jnp.maximum(magnitudes, pltpu.roll(magnitudes, OWNED, 1))
    return jnp.ceil(jnp.log2(jnp.maximum(most, 1e-30)) + 0.001)


def whole(values):
    return jnp.round(values).astype(I32).astype(jnp.int16)


HIST_COST = pl.CostEstimate(
    flops=2 * ROW_DEV * HALF * BINS * 256, bytes_accessed=8 << 20, transcendentals=0
)


def own_sums(core, codes, grads, weights, leaf):
    ins = [codes, grads, weights, leaf]
    return pl.pallas_call(
        own_kernel,
        grid=(PAIRS // UNROLL,),
        in_specs=[pl.BlockSpec(memory_space=pltpu.SMEM)]
        + [pl.BlockSpec(memory_space=pl.ANY)] * len(ins),
        out_specs=pl.BlockSpec((2 * UNROLL, SENT, HALF), lambda i: (i, 0, 0)),
        out_shape=jax.ShapeDtypeStruct((BINS, SENT, HALF), F32),
        scratch_shapes=[pltpu.VMEM((ROW_DEV, HALF), I32)]
        + [pltpu.VMEM(a.shape, a.dtype) for a in ins[1:]]
        + [
            pltpu.VMEM((ROW_DEV, HALF), BF16),
            pltpu.VMEM((COLS + TARGETS, ROW_DEV), BF16),
            pltpu.SemaphoreType.DMA((ROW_DEV // ROW_BLOCK + 3,)),
        ],
        compiler_params=params(36),
        cost_estimate=HIST_COST,
    )(core, *[in_hbm(a) for a in ins])


def both_sums(rows, sums):
    halved = (PEERS // 2, 2)
    out = pl.pallas_call(
        both_kernel,
        grid=(PAIRS // DEEPER,),
        in_specs=[
            pl.BlockSpec(rows.shape, lambda i: (0, 0), pipeline_mode=pl.Buffered(1)),
            pl.BlockSpec((2 * DEEPER, SENT, HALF), lambda i: (i, 0, 0)),
        ],
        out_specs=pl.BlockSpec((*halved, MESSAGE, COLS), lambda i: (0, 0, 0, 0)),
        out_shape=pltpu.HBM((*halved, MESSAGE, COLS), jnp.int16),
        scratch_shapes=[
            pltpu.VMEM((COLS + TARGETS, ROW_DEV), BF16),
            pltpu.VMEM((*halved, COLS, COLS), F32),
            pltpu.VMEM((*halved, 8, COLS), F32),
            pltpu.VMEM((COLS, HALF), F32),
            pltpu.VMEM((COLS, HALF), F32),
        ],
        compiler_params=params(40),
        cost_estimate=HIST_COST,
    )(rows, sums)
    return out.reshape(PEERS, MESSAGE, COLS)


def place_kernel(feature_ref, core_ref, bin_ref, aux_ref, codes_ref, keep_ref, give_ref):
    core = core_ref[0]
    grads, weights, leaf = split_aux(aux_ref[...].astype(F32))
    chosen = jnp.where(iota((8, 128), 1) == (feature_ref[0] & 127), 1.0, 0.0).astype(BF16)
    column = lax.dot_general(
        chosen,
        codes_ref[...].astype(F32).astype(BF16),
        (((1,), (1,)), ((), ())),
        preferred_element_type=F32,
    )[0:1]
    child = jnp.where(column > bin_ref[0].astype(F32), 1.0, 0.0)
    key = leaf * 2 + child
    keys = 2 * LEAVES
    hot = jnp.where(iota((keys, ROW_DEV), 0).astype(F32) == key, 1.0, 0.0)
    width = 256
    earlier = jnp.where(iota((width, width), 0) < iota((width, width), 1), 1.0, 0.0).astype(BF16)
    counts = jnp.zeros((keys, 1), F32)
    ranks = []
    for i in range(ROW_DEV // width):
        part = hot[:, i * width : (i + 1) * width]
        before = jnp.dot(part.astype(BF16), earlier, preferred_element_type=F32) + counts
        ranks.append(jnp.sum(part * before, axis=0, keepdims=True))
        counts = counts + jnp.sum(part, axis=1, keepdims=True)
    rank = jnp.concatenate(ranks, axis=1)
    sibling = iota((keys, ROW_DEV), 0).astype(F32) == leaf * 2
    first = jnp.sum(jnp.where(sibling, counts, 0.0), axis=0, keepdims=True)
    slot = (leaf * CAP + rank + child * first).astype(I32)
    dims = (((1,), (1,)), ((), ()))
    group = 128 // TARGETS
    tiled = jnp.concatenate([grads] * group, axis=0)
    values = jnp.where(iota((128, 1), 0) >> 4 == (slot & (group - 1)), tiled, 0.0).astype(BF16)
    lines = CAP // group
    line = iota((lines, 1), 0)
    for l in range(LEAVES):
        target = 2 * (l % 4) + (core if l < 4 else 1 - core)
        out_ref = keep_ref if l < 4 else give_ref
        pick = jnp.where(line == (slot >> 3) - target * lines, 1.0, 0.0).astype(BF16)
        moved = lax.dot_general(pick, values, dims, preferred_element_type=F32)
        out_ref[l % 4, :COLS, :] = moved.astype(BF16)
    lane_values = jnp.where(iota((128, 1), 0) == (slot & 127), weights, 0.0).astype(BF16)
    blocks = CAP // 128
    for l in range(LEAVES):
        target = 2 * (l % 4) + (core if l < 4 else 1 - core)
        out_ref = keep_ref if l < 4 else give_ref
        pick = jnp.where(iota((16, 1), 0) == (slot >> 7) - target * blocks, 1.0, 0.0)
        pick = jnp.where(iota((16, 1), 0) < blocks, pick, 0.0).astype(BF16)
        moved = lax.dot_general(pick, lane_values, dims, preferred_element_type=F32)
        out_ref[l % 4, COLS:, :] = moved.astype(BF16)


def place_rows(split_feature, core, split_bin, aux, codes):
    smem = pl.BlockSpec(memory_space=pltpu.SMEM)
    block = jax.ShapeDtypeStruct((LEAVES // 2, COLS + 16, 128), BF16)
    spec = pl.BlockSpec(block.shape, lambda i, feature: (0, 0, 0))
    return pl.pallas_call(
        place_kernel,
        grid_spec=pltpu.PrefetchScalarGridSpec(
            num_scalar_prefetch=1,
            grid=(1,),
            in_specs=[
                smem,
                smem,
                pl.BlockSpec(aux.shape, lambda i, feature: (0, 0)),
                pl.BlockSpec((ROW_DEV, 128), lambda i, feature: (0, feature[0] >> 7)),
            ],
            out_specs=[spec, spec],
        ),
        out_shape=[block, block],
        compiler_params=params(56),
        cost_estimate=pl.CostEstimate(
            flops=2 * LEAVES * CAP * ROW_DEV * 32, bytes_accessed=1 << 20, transcendentals=0
        ),
    )(split_feature, core, split_bin, aux, codes)


def deliver(keep, give, gains):
    core, chip = (lax.axis_index("grp_1"), lax.axis_index("grp_0"))
    got = lax.ppermute(give, "grp_1", [(0, 1), (1, 0)])
    first = jnp.where(core == 0, keep, got)
    second = jnp.where(core == 0, got, keep)
    blocks = jnp.stack([first, second], axis=1)
    arrived = []
    for s in range(4):
        block = lax.dynamic_index_in_dim(blocks, (chip + s) % 4, 0, keepdims=False)
        if s:
            block = lax.ppermute(block, "grp_0", [(i, (i + s) % 4) for i in range(4)])
        arrived.append(block)
    *arrived, gains = lax.optimization_barrier((*arrived, gains))
    turned = jnp.stack([arrived[0], arrived[3], arrived[2], arrived[1]] * 2)
    ordered = lax.dynamic_slice_in_dim(turned, (4 - chip) % 4, 4, 0)
    return ordered.reshape(8, COLS + 16, 128)


def gain_kernel(parts_ref, out_ref):
    upper = iota((8, COLS), 0) < OWNED

    def add_part(p, so_far):
        tail = parts_ref[p, COLS:, :].astype(I32).astype(F32)
        powers = jnp.exp2(tail[8:] - BITS)
        turned = pltpu.roll(powers, OWNED, 0)
        scale_g = jnp.where(upper, powers, turned)
        scale_w = jnp.where(upper, turned, powers)
        values = parts_ref[p, :COLS, :].astype(I32).astype(F32)
        added = [so_far[i] + values[i * 8 : (i + 1) * 8] * scale_g for i in range(PAIRS)]
        return (*added, so_far[PAIRS] + tail[:8] * scale_w)

    start = tuple(jnp.zeros((8, COLS), F32) for _ in range(PAIRS + 1))
    total = lax.fori_loop(0, PEERS, add_part, start, unroll=4)
    expand = jnp.where(
        iota((COLS, 1), 0) == iota((1, PAIRS * COLS), 1) >> 4, 1.0, 0.0
    )
    spread_w = jnp.dot(
        total[PAIRS], expand, preferred_element_type=F32, precision=lax.Precision.HIGHEST
    )
    grads = total[:PAIRS]
    weights = [spread_w[:, i * COLS : (i + 1) * COLS] for i in range(PAIRS)]
    row = iota((8, COLS), 0)
    even = row < OWNED

    def sides(values):
        swapped = [pltpu.roll(v, OWNED, 0) for v in values]
        both = [v + s for v, s in zip(values, swapped)]
        left, right = ([], [])
        below = jnp.zeros((8, COLS), F32)
        for v, b in zip(values, both):
            left.append(below + jnp.where(even, v, b))
            below = below + b
        above = jnp.zeros((8, COLS), F32)
        for s, b in zip(reversed(swapped), reversed(both)):
            right.append(above + jnp.where(even, s, 0.0))
            above = above + b
        return (left, right[::-1])

    left_g, right_g = sides(grads)
    left_w, right_w = sides(weights)
    place = (row & (OWNED - 1)) * BINS + (row >> 2)
    gains = jnp.zeros((8, COLS), F32)
    for i in range(PAIRS):
        x, y = (left_w[i] + 1.0, right_w[i] + 1.0)
        diff = left_g[i] * y - right_g[i] * x
        terms = diff * diff / (x * y * (x + y))
        sums = jnp.sum(terms, axis=1, keepdims=True)
        gains = gains + jnp.where(iota((8, COLS), 1) == place + 2 * i, sums, 0.0)
    gains = jnp.sum(gains, axis=0, keepdims=True) / (LEAVES * TARGETS)
    out_ref[...] = jnp.broadcast_to(gains[None], out_ref.shape)


def owned_gains(parts):
    shape = (2 * PEERS, 1, OWNED * BINS)
    return pl.pallas_call(
        gain_kernel,
        out_shape=jax.ShapeDtypeStruct(shape, F32),
        in_specs=[pl.BlockSpec(parts.shape, lambda: (0, 0, 0))],
        out_specs=pl.BlockSpec(shape, lambda: (0, 0, 0)),
        compiler_params=params(16),
    )(parts)


def close_kernel(group_ref, gains_ref, table_ref, best_ref):
    group = group_ref[0]
    first = (group & 1) * 64 + ((group & 7) >> 1) * 2 + (group >> 3)
    for i in range(8):
        table_ref[i] = gains_ref[first + 8 * i]
    highest = jnp.max(gains_ref[...], axis=0)
    best_ref[...] = jnp.max(highest, axis=1, keepdims=True)


def close(group, gains):
    return pl.pallas_call(
        close_kernel,
        out_shape=[
            jax.ShapeDtypeStruct((8, 1, OWNED * BINS), F32),
            jax.ShapeDtypeStruct((1, 1), F32),
        ],
        in_specs=[
            pl.BlockSpec(memory_space=pltpu.SMEM),
            pl.BlockSpec(gains.shape, lambda: (0, 0, 0)),
        ],
        out_specs=[
            pl.BlockSpec((8, 1, OWNED * BINS), lambda: (0, 0, 0)),
            pl.BlockSpec((1, 1), lambda: (0, 0)),
        ],
        compiler_params=params(4),
    )(group, gains)


def exchange(blocks, axis):
    return lax.all_to_all(blocks, axis, split_axis=0, concat_axis=0, tiled=True)


def shards(bin_codes, leaf_index, gradients, row_weights, split_feature, split_bin):
    core = lax.axis_index("grp_1").astype(I32).reshape(1)
    values = (gradients.T, row_weights.reshape(ROW_DEV // 128, 128), leaf_index.reshape(1, ROW_DEV))
    send, aux = prep(core, bin_codes, *values)
    other = lax.ppermute(send, "grp_1", [(0, 1), (1, 0)])
    sums = both_sums(other, own_sums(core, bin_codes, *values))
    arrived = exchange(sums, CHIPS)
    aux, unused = lax.optimization_barrier((aux, sums))
    gains = owned_gains(arrived)
    moved = deliver(*place_rows(split_feature, core, split_bin, aux, bin_codes), gains)
    everyone = exchange(gains, ROWS_GRP)
    table, best = close(lax.axis_index(ROWS).astype(I32).reshape(1), everyone)
    table, best = (table.reshape(-1), best.reshape(1))
    moved_gradients = moved[:, :COLS].reshape(1, -1)
    moved_weights = moved[:, COLS : COLS + 8].reshape(1, -1)
    return (table, best, moved_gradients, moved_weights)


def solution(mesh):
    torus = Mesh(mesh.devices.reshape(4, 4, 4, 2), ("rows_0", "rows_1", "grp_0", "grp_1"))
    in_specs = (P(ROWS_GRP, None), P(ROWS_GRP, None), P(ROWS_GRP, None), P(ROWS_GRP), P(), P())
    out_specs = (P(ROWS), P(), P(ROWS_GRP, None), P(ROWS_GRP, None))
    return jax.shard_map(
        shards, mesh=torus, in_specs=in_specs, out_specs=out_specs, check_vma=False
    )
```
